768 devices in a mesh: row: 12 (over x, z_lo), col: 64 (over y, z_hi, core).
Axes of the slice: x: 4, y: 8, z: 12 (z_hi: 4, z_lo: 3; z = z_hi * 3 + z_lo), core: 2. Of those that a mesh axis runs over, the one named last changes fastest.
Arguments:
- band_vectors: float32 [1024, 165888], P('col', 'row'), may hold values from -6 to 6
- bulge_vectors: float32 [12, 24, 256], P('row'), may hold values from -6 to 6
- counts: int32 [12], P('row'), may hold values from 6 to 24, as said below
- offsets: int32 [12, 24], P('row'), may hold values from 0 to 13568, as said below
- panel_vectors: bfloat16 [165888, 256], P(('row', 'col')), may hold values from -6 to 6
- factor: float32 [256, 256], replicated, as said below
- atom_slot: int32 [12, 4608], P('row'), may hold values from 0 to 4607, each once within a row
- isotope: int32 [55296], P('row'), may hold values from 0 to 15
- mass_table: float32 [16], replicated, may hold values from 1 to 240
Outputs:
- modes: float32 [1024, 165888], P('col', 'row')
The draws below stay inside these ranges and needn't reach their ends.
Inputs may be any that keep to these rules, and one draw needn't show every extreme that they name: The first counts[r] slots of row block r are used; some block uses all 24. The offsets of one row block differ from one another by at most 64. factor is upper triangular. Each row of atom_slot is a permutation.
All inputs are finite; a program needn't handle non-finite values.
Results may differ from the reference program's by a relative error of at most 0.0003.
Values may be sent and summed in bfloat16 or wider, within the bound.
No kernel may reach another device: no remote copies, remote signals or barrier semaphores. Data moves between devices by JAX's collectives and lax.ppermute only.
A program may use at most 64 MiB of HBM per device.

```python
import math
import jax
import jax.numpy as jnp
import numpy as np
from jax import lax

W = 256
NB = 128
K_MAX = 24
ISO = 16
BLK_DEV = 108
R_DEV = 13824
N = 165888
ATOM_DEV = 4608
ATOMS = 55296
M = 1024
N_ROW = 12


def draw_counts(key, part):
    base = jax.random.randint(jax.random.fold_in(key, 11), (N_ROW,), K_MAX // 4, K_MAX + 1)
    where = jax.random.randint(jax.random.fold_in(key, 12), (), 0, N_ROW)
    return base.at[where].set(K_MAX).astype(jnp.int32)


def draw_offsets(key, part):
    key = jax.random.fold_in(key, 31)
    spread = W // 4
    top = R_DEV - W - spread
    bases = jax.random.randint(jax.random.fold_in(key, 1), (N_ROW,), 0, top + 1)
    jitter = jax.random.randint(jax.random.fold_in(key, 2), (N_ROW, K_MAX), 0, spread + 1)
    low_block = jax.random.randint(jax.random.fold_in(key, 3), (), 0, N_ROW)
    step = jax.random.randint(jax.random.fold_in(key, 4), (), 1, max(N_ROW, 2))
    high_block = (low_block + step) % N_ROW
    bases = bases.at[low_block].set(0)
    bases = bases.at[high_block].set(top)
    jitter = jitter.at[low_block, 0].set(0)
    jitter = jitter.at[low_block, K_MAX - 1].set(spread)
    jitter = jitter.at[high_block, 0].set(spread)
    return (bases[:, None] + jitter).astype(jnp.int32)


def draw_factor(key, part):
    first = jax.random.fold_in(key, 21)
    second = jax.random.fold_in(key, 22)
    upper = jax.random.normal(first, (W, W), jnp.float32)
    diagonal = jax.random.uniform(second, (W,), jnp.float32, 2.0, 4.0)
    whole = jnp.triu(upper, 1) + jnp.diag(diagonal)
    return (whole / N).astype(jnp.float32)


def place_ends(values, rng, low, top_value):
    place = [jax.random.randint(jax.random.fold_in(rng, axis), (), 0, length) for axis, length in enumerate(values.shape)]
    longest = values.shape.index(max(values.shape))
    beside = place[:longest] + [(place[longest] + 1) % values.shape[longest]] + place[longest + 1:]
    return values.at[tuple(place)].set(low).at[tuple(beside)].set(top_value)


def levels(rng, shape, cuts, low, top_value):
    loudness = 1.0
    for dim, shards_of in cuts:
        draws = jax.random.uniform(jax.random.fold_in(jax.random.fold_in(rng, 6), dim), (shards_of,), jnp.float32, low / len(cuts), top_value / len(cuts))
        loudness = loudness * jnp.repeat(jnp.exp(draws), shape[dim] // shards_of).reshape((-1,) + (1,) * (len(shape) - 1 - dim))
    return loudness


def rank_table(amount, skew):
    weights = [(1 << 20) // math.isqrt(rank ** skew) + 1 for rank in range(1, amount + 1)]
    scale = 1 + sum(weights) // (1 << 30)
    return np.cumsum(np.array([max(1, weight // scale) for weight in weights]))


def ranked_ids(rng, extent, count, slope):
    grid = rank_table(count, slope)
    pick = jax.random.randint(jax.random.fold_in(rng, 1), extent, 0, int(grid[count - 1]))
    grade = jnp.searchsorted(jnp.asarray(grid, jnp.int32), pick, side="right")
    return jax.random.permutation(jax.random.fold_in(rng, 2), count)[grade].astype(jnp.int32)


def normal_values(key, extent, scale, reach, pieces=(), kind=jnp.bfloat16):
    result = scale * jax.random.normal(key, extent, jnp.float32)
    if pieces:
        result = result * levels(key, extent, pieces, -0.22, 0.18)
    return jnp.clip(result, -reach, reach).astype(kind)


def setup_inputs(seed: int = 0) -> dict:
    splits = jax.random.split(jax.random.key(seed), 10)
    band_vectors = normal_values(splits[0], (M, N), 1.0, 6.0, ((0, 64), (1, 12)), jnp.float32)
    bulge_vectors = normal_values(splits[1], (N_ROW, K_MAX, W), 1.0, 6.0, ((0, 12),), jnp.float32)
    counts = draw_counts(jax.random.fold_in(splits[9], 71), 0)
    offsets = draw_offsets(jax.random.fold_in(splits[9], 71), 0)
    panel_vectors = normal_values(splits[4], (N, W), 1.0, 6.0, ((0, 768),))
    factor = draw_factor(jax.random.fold_in(splits[9], 71), 0)
    atom_slot = jax.vmap(lambda own: jax.random.permutation(own, ATOM_DEV))(jax.random.split(splits[6], N_ROW)).reshape((N_ROW, ATOM_DEV)).astype(jnp.int32)
    isotope = place_ends(ranked_ids(splits[7], (ATOMS,), ISO, 2), jax.random.fold_in(splits[7], 3), 0, ISO - 1).astype(jnp.int32)
    mass_table = jnp.clip(jnp.exp(jax.random.uniform(splits[8], (ISO,), jnp.float32, math.log(1.0), math.log(240.0))), 1.0, 240.0)
    return dict(band_vectors=band_vectors, bulge_vectors=bulge_vectors, counts=counts, offsets=offsets, panel_vectors=panel_vectors, factor=factor, atom_slot=atom_slot, isotope=isotope, mass_table=mass_table)


HIGH = lax.Precision.HIGHEST

def chase(block, vectors, count, offsets):
    width = vectors.shape[1]

    def apply(slot, current):
        vector = vectors[slot]
        scaling = 2.0 / (jnp.sum(vector * vector) + 1e-06)
        start = offsets[slot].astype(jnp.int32)
        window = lax.dynamic_slice_in_dim(current, start, width, 1)
        inner = jnp.dot(window, vector, precision=HIGH)
        moved = window - scaling * inner[:, None] * vector[None, :]
        kept = jnp.where(slot < count, moved, window)
        return lax.dynamic_update_slice_in_dim(current, kept, start, 1)
    return lax.fori_loop(0, vectors.shape[0], apply, block)

def chase_item(item):
    return chase(item[0], item[1], item[2], item[3])

def reference(band_vectors, bulge_vectors, counts, offsets, panel_vectors, factor, atom_slot, isotope, mass_table):
    blocks = band_vectors.reshape(M, N_ROW, R_DEV).transpose(1, 0, 2)
    chased_blocks = lax.map(chase_item, (blocks, bulge_vectors, counts, offsets))
    chased = chased_blocks.transpose(1, 0, 2).reshape(M, N)
    wide = panel_vectors.astype(jnp.float32)
    projected = jnp.dot(chased, wide, precision=HIGH)
    factored = jnp.dot(projected, factor.T, precision=HIGH)
    updated = chased - jnp.dot(factored, wide.T, precision=HIGH)
    ordered = updated.reshape(M, N_ROW, BLK_DEV, NB).transpose(0, 2, 1, 3).reshape(M, N)
    local = (3 * atom_slot[:, :, None] + jnp.arange(3, dtype=jnp.int32)[None, None, :]).reshape(N_ROW, R_DEV)
    rows = (local + (jnp.arange(N_ROW, dtype=jnp.int32) * R_DEV)[:, None]).reshape(N).astype(jnp.int32)
    picked = jnp.take(ordered, rows, axis=1)
    weight = 1.0 / jnp.sqrt(mass_table)
    scale = jnp.repeat(weight[isotope], 3)
    return picked * scale[None, :]
```

```python
import functools

import jax
import jax.numpy as jnp
from jax import lax
from jax.experimental import pallas as pl
from jax.experimental.pallas import tpu as pltpu
from jax.sharding import PartitionSpec as P

NB = 128
HIGH = lax.Precision.HIGHEST
VMEM = pltpu.VMEM
SMEM = pltpu.SMEM
LIMIT = 48 * 1024 * 1024


def params(*semantics):
    return pltpu.CompilerParams(
        vmem_limit_bytes=LIMIT, dimension_semantics=semantics or None
    )


def parts_of(value, amount):
    parts = []
    for _ in range(amount):
        part = value.astype(jnp.bfloat16)
        parts.append(part)
        value = value - part.astype(jnp.float32)
    return jnp.concatenate(parts, axis=0)


def sum_parts(value, amount):
    rows = value.shape[0] // amount
    total = value[(amount - 1) * rows :]
    for index in reversed(range(amount - 1)):
        total = total + value[index * rows : (index + 1) * rows]
    return total


def chase_kernel(counts, offsets, band, vectors, out):
    slots, width = vectors.shape
    stored = band.shape[1]
    span = 2 * width
    low = offsets[0, 0]
    for slot in range(1, slots):
        low = jnp.minimum(low, offsets[0, slot])
    base = jnp.minimum((low // NB) * NB, stored - span)
    base = pl.multiple_of(base, NB)
    out[...] = band[...]
    window = band[:, pl.ds(base, span)]
    every = vectors[...]
    scaling = 2.0 / (jnp.sum(every * every, axis=1, keepdims=True) + 1e-06)
    for slot in range(slots):
        row = jnp.concatenate(
            [every[slot : slot + 1], jnp.zeros((1, span - width), jnp.float32)], axis=1
        )
        row = jnp.broadcast_to(row, (8, span))
        row = pltpu.roll(row, offsets[0, slot] - base, 1)
        row = jnp.concatenate([row] * (band.shape[0] // 8), axis=0)
        inner = jnp.sum(window * row, axis=1, keepdims=True)
        factor = jnp.where(slot < counts[0], scaling[slot : slot + 1], 0.0)
        window = window - (factor * inner) * row
    out[:, pl.ds(base, span)] = window


def chase(band, vectors, counts, offsets):
    return pl.pallas_call(
        chase_kernel,
        out_shape=jax.ShapeDtypeStruct(band.shape, jnp.float32),
        in_specs=[
            pl.BlockSpec(memory_space=SMEM),
            pl.BlockSpec(memory_space=SMEM),
            pl.BlockSpec(memory_space=VMEM),
            pl.BlockSpec(memory_space=VMEM),
        ],
        out_specs=pl.BlockSpec(memory_space=VMEM),
        compiler_params=params(),
        name="chase",
    )(counts, offsets, band, vectors)


def project_kernel(chased, panel, out, total):
    step = pl.program_id(0)
    product = jnp.dot(
        parts_of(chased[...], 3), panel[...], preferred_element_type=jnp.float32
    )
    before = jnp.where(step == 0, 0.0, total[...])
    done = before + sum_parts(product, 3)
    total[...] = done

    @pl.when(step == pl.num_programs(0) - 1)
    def _():
        for index in range(out.shape[0]):
            out[index] = done


def project(chased, panel, copies):
    rows, stored = chased.shape
    width = panel.shape[1]
    chunk = stored // 6
    return pl.pallas_call(
        project_kernel,
        grid=(stored // chunk,),
        out_shape=jax.ShapeDtypeStruct((copies, rows, width), jnp.float32),
        in_specs=[
            pl.BlockSpec((rows, chunk), lambda i: (0, i)),
            pl.BlockSpec((chunk, width), lambda i: (i, 0)),
        ],
        out_specs=pl.BlockSpec((copies, rows, width), lambda i: (0, 0, 0)),
        scratch_shapes=[pltpu.VMEM((rows, width), jnp.float32)],
        compiler_params=params("arbitrary"),
        name="project",
    )(chased, panel)


def update_kernel(shares, factor, chased, panel, out, factored):
    @pl.when(pl.program_id(0) == 0)
    def _():
        projected = jnp.sum(shares[...], axis=0)
        product = lax.dot_general(
            projected,
            factor[...],
            (((1,), (1,)), ((), ())),
            precision=HIGH,
            preferred_element_type=jnp.float32,
        )
        factored[...] = parts_of(product, 3)

    term = lax.dot_general(
        factored[...],
        panel[...],
        (((1,), (1,)), ((), ())),
        preferred_element_type=jnp.float32,
    )
    value = chased[...] - sum_parts(term, 3)
    for index in range(out.shape[0]):
        out[index] = value[:, index * NB : (index + 1) * NB]


def update(shares, factor, chased, panel):
    rows, stored = chased.shape
    width = panel.shape[1]
    chunk = stored // 6
    blocks = chunk // NB
    return pl.pallas_call(
        update_kernel,
        grid=(stored // chunk,),
        out_shape=jax.ShapeDtypeStruct((stored // NB, rows, NB), jnp.float32),
        in_specs=[
            pl.BlockSpec(shares.shape, lambda i: (0, 0, 0)),
            pl.BlockSpec(factor.shape, lambda i: (0, 0)),
            pl.BlockSpec((rows, chunk), lambda i: (0, i)),
            pl.BlockSpec((chunk, width), lambda i: (i, 0)),
        ],
        out_specs=pl.BlockSpec((blocks, rows, NB), lambda i: (i, 0, 0)),
        scratch_shapes=[pltpu.VMEM((3 * rows, width), jnp.bfloat16)],
        compiler_params=params("arbitrary"),
        name="update",
    )(shares, factor, chased, panel)


def reorder_kernel(slots, table, isotope, blocks, out, triples, picked):
    sources, depth, rows, _ = blocks.shape
    groups = out.shape[1] // (3 * NB)
    here = lax.broadcasted_iota(jnp.int32, (3 * NB, 3 * NB), 0)
    there = lax.broadcasted_iota(jnp.int32, (3 * NB, 3 * NB), 1)
    spread = (here == 3 * (there % NB) + there // NB).astype(jnp.bfloat16)
    closed = (there == 3 * (here % NB) + here // NB).astype(jnp.bfloat16)

    kind = isotope[...]
    mass = jnp.full(kind.shape, 1.0, jnp.float32)
    for index in range(table.shape[0]):
        mass = jnp.where(kind == index, table[index], mass)
    scale = 1.0 / jnp.sqrt(mass)

    per = sources // 3
    for group in range(groups):
        b, q = group // per, group % per
        wide = jnp.concatenate([blocks[3 * q + k, b] for k in range(3)], axis=1)
        apart = sum_parts(
            jnp.dot(parts_of(wide, 2), spread, preferred_element_type=jnp.float32), 2
        )
        tall = jnp.concatenate(
            [apart[:, c * NB : (c + 1) * NB] for c in range(3)]
            + [jnp.zeros((NB - 3 * rows, NB), jnp.float32)],
            axis=0,
        )
        triples[group * NB : (group + 1) * NB, :] = tall.T

    unroll = 32

    def pick(step, carry):
        start = pl.multiple_of(step * unroll, unroll)
        for index in range(unroll):
            slot = slots[0, start + index]
            picked[pl.ds(start + index, 1), :] = triples[pl.ds(slot, 1), :]
        return carry

    lax.fori_loop(0, slots.shape[1] // unroll, pick, 0)

    for group in range(groups):
        tall = picked[group * NB : (group + 1) * NB, :].T
        factor = scale[group : group + 1, :]
        wide = jnp.concatenate(
            [tall[c * rows : (c + 1) * rows] * factor for c in range(3)], axis=1
        )
        out[:, group * 3 * NB : (group + 1) * 3 * NB] = sum_parts(
            jnp.dot(parts_of(wide, 2), closed, preferred_element_type=jnp.float32), 2
        )


def reorder(blocks, slots, isotope, table):
    sources, depth, rows, _ = blocks.shape
    stored = sources * depth * NB
    atoms = stored // 3
    return pl.pallas_call(
        reorder_kernel,
        out_shape=jax.ShapeDtypeStruct((rows, stored), jnp.float32),
        in_specs=[
            pl.BlockSpec(memory_space=SMEM),
            pl.BlockSpec(memory_space=SMEM),
            pl.BlockSpec(memory_space=VMEM),
            pl.BlockSpec(memory_space=VMEM),
        ],
        out_specs=pl.BlockSpec(memory_space=VMEM),
        scratch_shapes=[
            pltpu.VMEM((atoms, NB), jnp.float32),
            pltpu.VMEM((atoms, NB), jnp.float32),
        ],
        compiler_params=params(),
        name="reorder",
    )(slots, table, isotope.reshape(-1, NB), blocks)


def exchange(value):
    return lax.all_to_all(value, "row", split_axis=0, concat_axis=0, tiled=True)


def per_device(
    band_vectors,
    bulge_vectors,
    counts,
    offsets,
    panel_vectors,
    factor,
    atom_slot,
    isotope,
    mass_table,
):
    row_count = lax.axis_size("row")
    whole = lax.all_gather(panel_vectors, "col", axis=0, tiled=True)
    chased = chase(band_vectors, bulge_vectors[0], counts, offsets)
    shares = exchange(project(chased, whole, row_count))
    updated = update(shares, factor, chased, whole)
    rows = updated.shape[1]
    moved = exchange(updated.reshape(row_count, -1, rows, NB))
    return reorder(moved, atom_slot, isotope, mass_table)


def solution(mesh):
    in_specs = (
        P("col", "row"),
        P("row", None, None),
        P("row"),
        P("row", None),
        P(("row", "col"), None),
        P(),
        P("row", None),
        P("row"),
        P(),
    )
    out_specs = P("col", "row")
    return jax.shard_map(
        per_device, mesh=mesh, in_specs=in_specs, out_specs=out_specs, check_vma=False
    )
```

```python
import jax
import jax.numpy as jnp
from jax import lax
from jax.experimental import pallas as pl
from jax.experimental.pallas import tpu as pltpu
from jax.sharding import Mesh
from jax.sharding import PartitionSpec as P

NB = 128
HIGH = lax.Precision.HIGHEST
VMEM = pltpu.VMEM
SMEM = pltpu.SMEM
LIMIT = 48 * 1024 * 1024


def params(*semantics):
    return pltpu.CompilerParams(
        vmem_limit_bytes=LIMIT, dimension_semantics=semantics or None
    )


def parts_of(value, amount):
    parts = []
    for _ in range(amount):
        part = value.astype(jnp.bfloat16)
        parts.append(part)
        value = value - part.astype(jnp.float32)
    return jnp.concatenate(parts, axis=0)


def sum_parts(value, amount):
    rows = value.shape[0] // amount
    total = value[(amount - 1) * rows :]
    for index in reversed(range(amount - 1)):
        total = total + value[index * rows : (index + 1) * rows]
    return total


def chase_kernel(counts, offsets, band, vectors, out):
    slots, width = vectors.shape
    stored = band.shape[1]
    span = 2 * width
    low = offsets[0, 0]
    for slot in range(1, slots):
        low = jnp.minimum(low, offsets[0, slot])
    base = jnp.minimum((low // NB) * NB, stored - span)
    base = pl.multiple_of(base, NB)
    out[...] = band[...]
    window = band[:, pl.ds(base, span)]
    every = vectors[...]
    scaling = 2.0 / (jnp.sum(every * every, axis=1, keepdims=True) + 1e-06)
    for slot in range(slots):
        row = jnp.concatenate(
            [every[slot : slot + 1], jnp.zeros((1, span - width), jnp.float32)], axis=1
        )
        row = jnp.broadcast_to(row, (8, span))
        row = pltpu.roll(row, offsets[0, slot] - base, 1)
        row = jnp.concatenate([row] * (band.shape[0] // 8), axis=0)
        inner = jnp.sum(window * row, axis=1, keepdims=True)
        factor = jnp.where(slot < counts[0], scaling[slot : slot + 1], 0.0)
        window = window - (factor * inner) * row
    out[:, pl.ds(base, span)] = window


def chase(band, vectors, counts, offsets):
    return pl.pallas_call(
        chase_kernel,
        out_shape=jax.ShapeDtypeStruct(band.shape, jnp.float32),
        in_specs=[
            pl.BlockSpec(memory_space=SMEM),
            pl.BlockSpec(memory_space=SMEM),
            pl.BlockSpec(memory_space=VMEM),
            pl.BlockSpec(memory_space=VMEM),
        ],
        out_specs=pl.BlockSpec(memory_space=VMEM),
        compiler_params=params(),
        name="chase",
    )(counts, offsets, band, vectors)


def chunk_of(stored):
    return 18 * NB if stored % (18 * NB) == 0 else 9 * NB


def project_kernel(core, chased, other, panel, out, total):
    step = pl.program_id(0)
    rows = chased.shape[0]
    both = jnp.concatenate([chased[...], other[...]], axis=0)
    product = jnp.dot(
        parts_of(both, 3), panel[...], preferred_element_type=jnp.float32
    )
    before = jnp.where(step == 0, 0.0, total[...])
    done = before + sum_parts(product, 3)
    total[...] = done

    @pl.when(step == pl.num_programs(0) - 1)
    def _():
        first = core[0] == 0
        mine, its = done[:rows], done[rows:]
        low, high = jnp.where(first, mine, its), jnp.where(first, its, mine)
        for index in range(out.shape[0] // 2):
            out[2 * index] = low
            out[2 * index + 1] = high


def project(core, chased, other, panel, copies):
    rows, stored = chased.shape
    width = panel.shape[1]
    chunk = chunk_of(stored)
    return pl.pallas_call(
        project_kernel,
        grid=(stored // chunk,),
        out_shape=jax.ShapeDtypeStruct((2 * copies, rows, width), jnp.float32),
        in_specs=[
            pl.BlockSpec(memory_space=SMEM),
            pl.BlockSpec((rows, chunk), lambda i: (0, i)),
            pl.BlockSpec((rows, chunk), lambda i: (0, i)),
            pl.BlockSpec((chunk, width), lambda i: (i, 0)),
        ],
        out_specs=pl.BlockSpec((2 * copies, rows, width), lambda i: (0, 0, 0)),
        scratch_shapes=[pltpu.VMEM((2 * rows, width), jnp.float32)],
        compiler_params=params("arbitrary"),
        name="project",
    )(core, chased, other, panel)


def update_kernel(core, shares, factor, chased, panel, panel_other, out, factored):
    @pl.when(pl.program_id(0) == 0)
    def _():
        low, high = shares[0], shares[1]
        for index in range(1, shares.shape[0] // 2):
            low = low + shares[2 * index]
            high = high + shares[2 * index + 1]
        product = lax.dot_general(
            jnp.concatenate([low, high], axis=1),
            factor[...],
            (((1,), (1,)), ((), ())),
            precision=HIGH,
            preferred_element_type=jnp.float32,
        )
        half = product.shape[1] // 2
        turned = jnp.concatenate([product[:, half:], product[:, :half]], axis=1)
        factored[...] = parts_of(jnp.where(core[0] == 0, product, turned), 3)

    term = lax.dot_general(
        factored[...],
        jnp.concatenate([panel[...], panel_other[...]], axis=1),
        (((1,), (1,)), ((), ())),
        preferred_element_type=jnp.float32,
    )
    value = chased[...] - sum_parts(term, 3)
    for index in range(out.shape[0]):
        out[index] = value[:, index * NB : (index + 1) * NB]


def update(core, shares, factor, chased, panel, panel_other):
    rows, stored = chased.shape
    half = panel.shape[1]
    chunk = chunk_of(stored)
    return pl.pallas_call(
        update_kernel,
        grid=(stored // chunk,),
        out_shape=jax.ShapeDtypeStruct((stored // NB, rows, NB), jnp.float32),
        in_specs=[
            pl.BlockSpec(memory_space=SMEM),
            pl.BlockSpec(shares.shape, lambda i: (0, 0, 0)),
            pl.BlockSpec(factor.shape, lambda i: (0, 0)),
            pl.BlockSpec((rows, chunk), lambda i: (0, i)),
            pl.BlockSpec((chunk, half), lambda i: (i, 0)),
            pl.BlockSpec((chunk, half), lambda i: (i, 0)),
        ],
        out_specs=pl.BlockSpec((chunk // NB, rows, NB), lambda i: (i, 0, 0)),
        scratch_shapes=[pltpu.VMEM((3 * rows, 2 * half), jnp.bfloat16)],
        compiler_params=params("arbitrary"),
        name="update",
    )(core, shares, factor, chased, panel, panel_other)


def reorder_kernel(slots, table, isotope, blocks, out, triples, picked):
    sources, depth, rows, _ = blocks.shape
    groups = out.shape[1] // (3 * NB)
    here = lax.broadcasted_iota(jnp.int32, (3 * NB, 3 * NB), 0)
    there = lax.broadcasted_iota(jnp.int32, (3 * NB, 3 * NB), 1)
    spread = (here == 3 * (there % NB) + there // NB).astype(jnp.bfloat16)
    closed = (there == 3 * (here % NB) + here // NB).astype(jnp.bfloat16)

    kind = isotope[...]
    mass = jnp.full(kind.shape, 1.0, jnp.float32)
    for index in range(table.shape[0]):
        mass = jnp.where(kind == index, table[index], mass)
    scale = 1.0 / jnp.sqrt(mass)

    per = sources // 3
    for group in range(groups):
        b, q = group // per, group % per
        wide = jnp.concatenate([blocks[3 * q + k, b] for k in range(3)], axis=1)
        apart = sum_parts(
            jnp.dot(parts_of(wide, 2), spread, preferred_element_type=jnp.float32), 2
        )
        tall = jnp.concatenate(
            [apart[:, c * NB : (c + 1) * NB] for c in range(3)]
            + [jnp.zeros((NB - 3 * rows, NB), jnp.float32)],
            axis=0,
        )
        triples[group * NB : (group + 1) * NB, :] = tall.T

    unroll = 32

    def pick(step, carry):
        start = pl.multiple_of(step * unroll, unroll)
        for index in range(unroll):
            slot = slots[0, start + index]
            picked[pl.ds(start + index, 1), :] = triples[pl.ds(slot, 1), :]
        return carry

    lax.fori_loop(0, slots.shape[1] // unroll, pick, 0)

    for group in range(groups):
        tall = picked[group * NB : (group + 1) * NB, :].T
        factor = scale[group : group + 1, :]
        wide = jnp.concatenate(
            [tall[c * rows : (c + 1) * rows] * factor for c in range(3)], axis=1
        )
        out[:, group * 3 * NB : (group + 1) * 3 * NB] = sum_parts(
            jnp.dot(parts_of(wide, 2), closed, preferred_element_type=jnp.float32), 2
        )


def reorder(blocks, slots, isotope, table):
    sources, depth, rows, _ = blocks.shape
    stored = sources * depth * NB
    atoms = stored // 3
    return pl.pallas_call(
        reorder_kernel,
        out_shape=jax.ShapeDtypeStruct((rows, stored), jnp.float32),
        in_specs=[
            pl.BlockSpec(memory_space=SMEM),
            pl.BlockSpec(memory_space=SMEM),
            pl.BlockSpec(memory_space=VMEM),
            pl.BlockSpec(memory_space=VMEM),
        ],
        out_specs=pl.BlockSpec(memory_space=VMEM),
        scratch_shapes=[
            pltpu.VMEM((atoms, NB), jnp.float32),
            pltpu.VMEM((atoms, NB), jnp.float32),
        ],
        compiler_params=params(),
        name="reorder",
    )(slots, table, isotope.reshape(-1, NB), blocks)


ROW = ("x", "z_lo")
COL = ("y", "z_hi", "core")
SIZES = (4, 3, 8, 4, 2)


def exchange(value, axes):
    return lax.all_to_all(value, axes, split_axis=0, concat_axis=0, tiled=True)


def other_core(value):
    return lax.ppermute(value, "core", [(0, 1), (1, 0)])


def gather_half(panel):
    half = panel.shape[1] // 2
    first = lax.axis_index("core") == 0
    low, high = panel[:, :half], panel[:, half:]
    kept = jnp.where(first, low, high)
    got = other_core(jnp.where(first, high, low))
    pair = jnp.concatenate([jnp.where(first, kept, got), jnp.where(first, got, kept)])
    plane = lax.all_gather(pair, "z_hi", axis=0, tiled=True)
    return lax.all_gather(plane, "y", axis=0, tiled=True)


def per_device(
    band_vectors,
    bulge_vectors,
    counts,
    offsets,
    panel_vectors,
    factor,
    atom_slot,
    isotope,
    mass_table,
):
    row_count = lax.axis_size(ROW)
    core = lax.axis_index("core").reshape(1).astype(jnp.int32)
    panel = gather_half(panel_vectors)
    chased = chase(band_vectors, bulge_vectors[0], counts, offsets)
    other = other_core(chased)
    sums = project(core, chased, other, panel, row_count)
    panel_other = other_core(panel)
    shares = exchange(sums, ROW + ("core",))
    updated = update(core, shares, factor, chased, panel, panel_other)
    rows = updated.shape[1]
    moved = exchange(updated.reshape(row_count, -1, rows, NB), ROW)
    return reorder(moved, atom_slot, isotope, mass_table)


def solution(mesh):
    fine = Mesh(mesh.devices.reshape(SIZES), ROW + COL)
    in_specs = (
        P(COL, ROW),
        P(ROW, None, None),
        P(ROW),
        P(ROW, None),
        P(ROW + COL, None),
        P(),
        P(ROW, None),
        P(ROW),
        P(),
    )
    return jax.shard_map(
        per_device,
        mesh=fine,
        in_specs=in_specs,
        out_specs=P(COL, ROW),
        check_vma=False,
    )
```

```python
import jax
import jax.numpy as jnp
from jax import lax
from jax.experimental import pallas as pl
from jax.experimental.pallas import tpu as pltpu
from jax.sharding import Mesh
from jax.sharding import PartitionSpec as P

NB = 128
HIGH = lax.Precision.HIGHEST
VMEM = pltpu.VMEM
SMEM = pltpu.SMEM
LIMIT = 48 * 1024 * 1024


def cost(microseconds):
    return pl.CostEstimate(
        flops=0, bytes_accessed=int(3.0e6 * microseconds), transcendentals=0
    )


def params(*semantics):
    return pltpu.CompilerParams(
        vmem_limit_bytes=LIMIT, dimension_semantics=semantics or None
    )


def parts_of(value, amount):
    parts = []
    for _ in range(amount):
        part = value.astype(jnp.bfloat16)
        parts.append(part)
        value = value - part.astype(jnp.float32)
    return jnp.concatenate(parts, axis=0)


def sum_parts(value, amount):
    rows = value.shape[0] // amount
    total = value[(amount - 1) * rows :]
    for index in reversed(range(amount - 1)):
        total = total + value[index * rows : (index + 1) * rows]
    return total


def chase_kernel(counts, offsets, band, vectors, out):
    slots, width = vectors.shape
    stored = band.shape[1]
    span = 2 * width
    low = offsets[0, 0]
    for slot in range(1, slots):
        low = jnp.minimum(low, offsets[0, slot])
    base = jnp.minimum((low // NB) * NB, stored - span)
    base = pl.multiple_of(base, NB)
    out[...] = band[...]
    window = band[:, pl.ds(base, span)]
    every = vectors[...]
    scaling = 2.0 / (jnp.sum(every * every, axis=1, keepdims=True) + 1e-06)
    for slot in range(slots):
        row = jnp.concatenate(
            [every[slot : slot + 1], jnp.zeros((1, span - width), jnp.float32)], axis=1
        )
        row = jnp.broadcast_to(row, (8, span))
        row = pltpu.roll(row, offsets[0, slot] - base, 1)
        row = jnp.concatenate([row] * (band.shape[0] // 8), axis=0)
        inner = jnp.sum(window * row, axis=1, keepdims=True)
        factor = jnp.where(slot < counts[0], scaling[slot : slot + 1], 0.0)
        window = window - (factor * inner) * row
    out[:, pl.ds(base, span)] = window


def chase(band, vectors, counts, offsets):
    return pl.pallas_call(
        chase_kernel,
        out_shape=jax.ShapeDtypeStruct(band.shape, jnp.float32),
        in_specs=[
            pl.BlockSpec(memory_space=SMEM),
            pl.BlockSpec(memory_space=SMEM),
            pl.BlockSpec(memory_space=VMEM),
            pl.BlockSpec(memory_space=VMEM),
        ],
        out_specs=pl.BlockSpec(memory_space=VMEM),
        compiler_params=params(),
        cost_estimate=cost(4),
        name="chase",
    )(counts, offsets, band, vectors)


def chunk_of(stored):
    return 18 * NB if stored % (18 * NB) == 0 else 9 * NB


def project_kernel(core, chased, other, panel, out, total):
    step = pl.program_id(0)
    rows = chased.shape[0]
    both = jnp.concatenate([chased[...], other[...]], axis=0)
    product = jnp.dot(
        parts_of(both, 3), panel[...], preferred_element_type=jnp.float32
    )
    before = jnp.where(step == 0, 0.0, total[...])
    done = before + sum_parts(product, 3)
    total[...] = done

    @pl.when(step == pl.num_programs(0) - 1)
    def _():
        first = core[0] == 0
        mine, its = done[:rows], done[rows:]
        low, high = jnp.where(first, mine, its), jnp.where(first, its, mine)
        for index in range(out.shape[0] // 2):
            out[2 * index] = low
            out[2 * index + 1] = high


def project(core, chased, other, panel, copies):
    rows, stored = chased.shape
    width = panel.shape[1]
    chunk = chunk_of(stored)
    return pl.pallas_call(
        project_kernel,
        grid=(stored // chunk,),
        out_shape=jax.ShapeDtypeStruct((2 * copies, rows, width), jnp.float32),
        in_specs=[
            pl.BlockSpec(memory_space=SMEM),
            pl.BlockSpec((rows, chunk), lambda i: (0, i)),
            pl.BlockSpec((rows, chunk), lambda i: (0, i)),
            pl.BlockSpec((chunk, width), lambda i: (i, 0)),
        ],
        out_specs=pl.BlockSpec((2 * copies, rows, width), lambda i: (0, 0, 0)),
        scratch_shapes=[pltpu.VMEM((2 * rows, width), jnp.float32)],
        compiler_params=params("arbitrary"),
        cost_estimate=cost(4),
        name="project",
    )(core, chased, other, panel)


TOP = 32767.0
SHIFT = 16


def encode(blocks):
    lane = lax.broadcasted_iota(jnp.int32, blocks[0].shape, 1)
    largest = jnp.zeros_like(blocks[0])
    for index, block in enumerate(blocks):
        size = jnp.max(jnp.abs(block), axis=1, keepdims=True)
        largest = jnp.where(lane == index, size, largest)
    exponent = jnp.floor(jnp.log2(jnp.maximum(largest, 1e-36)))
    exponent = jnp.clip(exponent, -118.0, 118.0)
    down = jnp.exp2(-exponent)
    mantissa = jnp.maximum(jnp.ceil(largest * down * 64.0), 1.0)
    back = (64.0 * TOP) / mantissa
    codes = []
    for index, block in enumerate(blocks):
        code = (block * down[:, index : index + 1]) * back[:, index : index + 1]
        code = jnp.clip(jnp.round(code), -TOP, TOP)
        codes.append(code.astype(jnp.int32).astype(jnp.int16))
    count = len(blocks)
    beside = jnp.where(lane < count, exponent, 0.0)
    moved = pltpu.roll(mantissa, SHIFT, 1)
    beside = jnp.where((lane >= SHIFT) & (lane < SHIFT + count), moved, beside)
    codes.append(beside.astype(jnp.int32).astype(jnp.int16))
    return codes


def decode_scales(beside):
    value = beside.astype(jnp.int32).astype(jnp.float32)
    lane = lax.broadcasted_iota(jnp.int32, value.shape, 1)
    mantissa = pltpu.roll(value, NB - SHIFT, 1)
    return (mantissa / (64.0 * TOP)) * jnp.exp2(jnp.where(lane < SHIFT, value, 0.0))


def update_kernel(core, shares, factor, chased, panel, panel_other, out, factored):
    @pl.when(pl.program_id(0) == 0)
    def _():
        low, high = shares[0], shares[1]
        for index in range(1, shares.shape[0] // 2):
            low = low + shares[2 * index]
            high = high + shares[2 * index + 1]
        product = lax.dot_general(
            jnp.concatenate([low, high], axis=1),
            factor[...],
            (((1,), (1,)), ((), ())),
            precision=HIGH,
            preferred_element_type=jnp.float32,
        )
        half = product.shape[1] // 2
        turned = jnp.concatenate([product[:, half:], product[:, :half]], axis=1)
        factored[...] = parts_of(jnp.where(core[0] == 0, product, turned), 3)

    term = lax.dot_general(
        factored[...],
        jnp.concatenate([panel[...], panel_other[...]], axis=1),
        (((1,), (1,)), ((), ())),
        preferred_element_type=jnp.float32,
    )
    value = chased[...] - sum_parts(term, 3)
    depth = out.shape[1] - 1
    for where in range(out.shape[0]):
        first = where * depth
        codes = encode(
            [value[:, (first + b) * NB : (first + b + 1) * NB] for b in range(depth)]
        )
        for index, code in enumerate(codes):
            out[where, index] = code


def update(core, shares, factor, chased, panel, panel_other, row_count):
    rows, stored = chased.shape
    half = panel.shape[1]
    chunk = chunk_of(stored)
    depth = stored // (row_count * NB)
    parts = chunk // (depth * NB)
    return pl.pallas_call(
        update_kernel,
        grid=(stored // chunk,),
        out_shape=jax.ShapeDtypeStruct((row_count, depth + 1, rows, NB), jnp.int16),
        in_specs=[
            pl.BlockSpec(memory_space=SMEM),
            pl.BlockSpec(shares.shape, lambda i: (0, 0, 0)),
            pl.BlockSpec(factor.shape, lambda i: (0, 0)),
            pl.BlockSpec((rows, chunk), lambda i: (0, i)),
            pl.BlockSpec((chunk, half), lambda i: (i, 0)),
            pl.BlockSpec((chunk, half), lambda i: (i, 0)),
        ],
        out_specs=pl.BlockSpec((parts, depth + 1, rows, NB), lambda i: (i, 0, 0, 0)),
        scratch_shapes=[pltpu.VMEM((3 * rows, 2 * half), jnp.bfloat16)],
        compiler_params=params("arbitrary"),
        cost_estimate=cost(6),
        name="update",
    )(core, shares, factor, chased, panel, panel_other)


def reorder_kernel(slots, table, isotope, blocks, out, triples, picked):
    sources, rows = blocks.shape[0], blocks.shape[2]
    depth = blocks.shape[1] - 1
    scales = [decode_scales(blocks[source, depth]) for source in range(sources)]

    def block(source, b):
        code = blocks[source, b].astype(jnp.int32).astype(jnp.float32)
        return code * scales[source][:, b : b + 1]

    groups = out.shape[1] // (3 * NB)
    here = lax.broadcasted_iota(jnp.int32, (3 * NB, 3 * NB), 0)
    there = lax.broadcasted_iota(jnp.int32, (3 * NB, 3 * NB), 1)
    spread = (here == 3 * (there % NB) + there // NB).astype(jnp.bfloat16)
    closed = (there == 3 * (here % NB) + here // NB).astype(jnp.bfloat16)

    kind = isotope[...]
    mass = jnp.full(kind.shape, 1.0, jnp.float32)
    for index in range(table.shape[0]):
        mass = jnp.where(kind == index, table[index], mass)
    scale = 1.0 / jnp.sqrt(mass)

    per = sources // 3
    for group in range(groups):
        b, q = group // per, group % per
        wide = jnp.concatenate([block(3 * q + k, b) for k in range(3)], axis=1)
        apart = sum_parts(
            jnp.dot(parts_of(wide, 2), spread, preferred_element_type=jnp.float32), 2
        )
        tall = jnp.concatenate(
            [apart[:, c * NB : (c + 1) * NB] for c in range(3)]
            + [jnp.zeros((NB - 3 * rows, NB), jnp.float32)],
            axis=0,
        )
        triples[group * NB : (group + 1) * NB, :] = tall.T

    unroll = 32

    def pick(step, carry):
        start = pl.multiple_of(step * unroll, unroll)
        for index in range(unroll):
            slot = slots[0, start + index]
            picked[pl.ds(start + index, 1), :] = triples[pl.ds(slot, 1), :]
        return carry

    lax.fori_loop(0, slots.shape[1] // unroll, pick, 0)

    for group in range(groups):
        tall = picked[group * NB : (group + 1) * NB, :].T
        factor = scale[group : group + 1, :]
        wide = jnp.concatenate(
            [tall[c * rows : (c + 1) * rows] * factor for c in range(3)], axis=1
        )
        out[:, group * 3 * NB : (group + 1) * 3 * NB] = sum_parts(
            jnp.dot(parts_of(wide, 2), closed, preferred_element_type=jnp.float32), 2
        )


def reorder(blocks, slots, isotope, table):
    sources, rows = blocks.shape[0], blocks.shape[2]
    stored = sources * (blocks.shape[1] - 1) * NB
    atoms = stored // 3
    return pl.pallas_call(
        reorder_kernel,
        out_shape=jax.ShapeDtypeStruct((rows, stored), jnp.float32),
        in_specs=[
            pl.BlockSpec(memory_space=SMEM),
            pl.BlockSpec(memory_space=SMEM),
            pl.BlockSpec(memory_space=VMEM),
            pl.BlockSpec(memory_space=VMEM),
        ],
        out_specs=pl.BlockSpec(memory_space=VMEM),
        scratch_shapes=[
            pltpu.VMEM((atoms, NB), jnp.float32),
            pltpu.VMEM((atoms, NB), jnp.float32),
        ],
        compiler_params=params(),
        cost_estimate=cost(10),
        name="reorder",
    )(slots, table, isotope.reshape(-1, NB), blocks)


ROW = ("x", "z_lo")
COL = ("y", "z_hi", "core")
SIZES = (4, 3, 8, 4, 2)


def exchange(value, axes):
    return lax.all_to_all(value, axes, split_axis=0, concat_axis=0, tiled=True)


def other_core(value):
    return lax.ppermute(value, "core", [(0, 1), (1, 0)])


def gather_half(panel):
    half = panel.shape[1] // 2
    first = lax.axis_index("core") == 0
    low, high = panel[:, :half], panel[:, half:]
    kept = jnp.where(first, low, high)
    got = other_core(jnp.where(first, high, low))
    pair = jnp.concatenate([jnp.where(first, kept, got), jnp.where(first, got, kept)])
    plane = lax.all_gather(pair, "z_hi", axis=0, tiled=True)
    return lax.all_gather(plane, "y", axis=0, tiled=True)


def per_device(
    band_vectors,
    bulge_vectors,
    counts,
    offsets,
    panel_vectors,
    factor,
    atom_slot,
    isotope,
    mass_table,
):
    row_count = lax.axis_size(ROW)
    core = lax.axis_index("core").reshape(1).astype(jnp.int32)
    panel = gather_half(panel_vectors)
    chased = chase(band_vectors, bulge_vectors[0], counts, offsets)
    other = other_core(chased)
    panel, chased, other = lax.optimization_barrier((panel, chased, other))
    sums = project(core, chased, other, panel, row_count)
    panel_other = other_core(panel)
    shares = exchange(sums, ROW + ("core",))
    updated = update(core, shares, factor, chased, panel, panel_other, row_count)
    moved = exchange(updated, ROW)
    return reorder(moved, atom_slot, isotope, mass_table)


def solution(mesh):
    fine = Mesh(mesh.devices.reshape(SIZES), ROW + COL)
    in_specs = (
        P(COL, ROW),
        P(ROW, None, None),
        P(ROW),
        P(ROW, None),
        P(ROW + COL, None),
        P(),
        P(ROW, None),
        P(ROW),
        P(),
    )
    return jax.shard_map(
        per_device,
        mesh=fine,
        in_specs=in_specs,
        out_specs=P(COL, ROW),
        check_vma=False,
    )
```

```python
import functools

import jax
import jax.numpy as jnp
from jax import lax
from jax.experimental import pallas as pl
from jax.experimental.pallas import tpu as pltpu
from jax.sharding import Mesh
from jax.sharding import PartitionSpec as P

NB = 128
HIGH = lax.Precision.HIGHEST
VMEM = pltpu.VMEM
SMEM = pltpu.SMEM
LIMIT = 16 * 1024 * 1024


def cost(microseconds):
    return pl.CostEstimate(
        flops=0, bytes_accessed=int(3.0e6 * microseconds), transcendentals=0
    )


def params(*semantics):
    return pltpu.CompilerParams(
        vmem_limit_bytes=LIMIT, dimension_semantics=semantics or None
    )


def parts_of(value, amount):
    parts = []
    for _ in range(amount):
        part = value.astype(jnp.bfloat16)
        parts.append(part)
        value = value - part.astype(jnp.float32)
    return jnp.concatenate(parts, axis=0)


def sum_parts(value, amount):
    rows = value.shape[0] // amount
    total = value[(amount - 1) * rows :]
    for index in reversed(range(amount - 1)):
        total = total + value[index * rows : (index + 1) * rows]
    return total


def chase_kernel(counts, offsets, band, vectors, out, places):
    slots, width = vectors.shape
    stored = band.shape[1]
    span = 2 * width
    low = offsets[0, 0]
    for slot in range(1, slots):
        low = jnp.minimum(low, offsets[0, slot])
    base = jnp.minimum((low // NB) * NB, stored - span)
    base = pl.multiple_of(base, NB)
    out[...] = band[...]
    window = band[:, pl.ds(base, span)]
    every = vectors[...]
    scaling = 2.0 / (jnp.sum(every * every, axis=1, keepdims=True) + 1e-06)
    for slot in range(slots):
        row = jnp.concatenate(
            [every[slot : slot + 1], jnp.zeros((1, span - width), jnp.float32)], axis=1
        )
        row = jnp.broadcast_to(row, (8, span))
        row = pltpu.roll(row, offsets[0, slot] - base, 1)
        row = jnp.concatenate([row] * (band.shape[0] // 8), axis=0)
        inner = jnp.sum(window * row, axis=1, keepdims=True)
        factor = jnp.where(slot < counts[0], scaling[slot : slot + 1], 0.0)
        window = window - (factor * inner) * row
    out[:, pl.ds(base, span)] = window
    part = places.shape[2]
    for index in range(places.shape[0]):
        places[index] = out[:, index * part : (index + 1) * part]


def chase(band, vectors, counts, offsets, places):
    rows, stored = band.shape
    return pl.pallas_call(
        chase_kernel,
        out_shape=[
            jax.ShapeDtypeStruct(band.shape, jnp.float32),
            jax.ShapeDtypeStruct((places, rows, stored // places), jnp.float32),
        ],
        in_specs=[
            pl.BlockSpec(memory_space=SMEM),
            pl.BlockSpec(memory_space=SMEM),
            pl.BlockSpec(memory_space=VMEM),
            pl.BlockSpec(memory_space=VMEM),
        ],
        out_specs=[pl.BlockSpec(memory_space=VMEM)] * 2,
        compiler_params=params(),
        cost_estimate=cost(4),
        name="chase",
    )(counts, offsets, band, vectors)


def place_product(mine, its, source, part):
    both = jnp.concatenate([mine[source], its[source]], axis=0)
    flat = part.reshape(part.shape[0] * part.shape[1], part.shape[2])
    return jnp.dot(parts_of(both, 3), flat, preferred_element_type=jnp.float32)


def near_kernel(place, mine, its, *rest, steps):
    pieces, (out, whole) = rest[: len(steps)], rest[len(steps) :]
    count = whole.shape[0]
    done = jnp.zeros((3 * out.shape[0], out.shape[1]), jnp.float32)
    for piece, step in zip(pieces, steps):
        source = lax.rem(place[1] + step + count, count)
        part = piece[...]
        whole[source] = part
        done = done + place_product(mine, its, source, part)
    out[...] = sum_parts(done, 3)


def project_near(place, mine, its, pieces, steps):
    count, rows, _ = mine.shape
    shape = pieces[0].shape
    near = pl.BlockSpec(memory_space=VMEM)
    return pl.pallas_call(
        functools.partial(near_kernel, steps=steps),
        out_shape=[
            jax.ShapeDtypeStruct((2 * rows, shape[2]), jnp.float32),
            jax.ShapeDtypeStruct((count,) + shape, jnp.bfloat16),
        ],
        in_specs=[pl.BlockSpec(memory_space=SMEM)] + [near] * (2 + len(pieces)),
        out_specs=[near, near],
        compiler_params=params(),
        cost_estimate=cost(6),
        name="near",
    )(place, mine, its, *pieces)


def far_kernel(place, mine, its, before, low, high, _, out, whole):
    count = whole.shape[0]
    rows = before.shape[0] // 2
    source = lax.rem(place[1] + count // 2, count)
    part = jnp.concatenate([low[...], high[...]], axis=0)
    whole[source] = part
    product = place_product(mine, its, source, part)
    done = before[...] + sum_parts(product, 3)
    zero = place[0] == 0
    own, other = done[:rows], done[rows:]
    even, odd = jnp.where(zero, own, other), jnp.where(zero, other, own)
    for index in range(out.shape[0] // 2):
        out[2 * index] = even
        out[2 * index + 1] = odd


def project_far(place, mine, its, before, low, high, whole, copies):
    rows = mine.shape[1]
    near = pl.BlockSpec(memory_space=VMEM)
    return pl.pallas_call(
        far_kernel,
        out_shape=[
            jax.ShapeDtypeStruct((2 * copies, rows, whole.shape[3]), jnp.float32),
            jax.ShapeDtypeStruct(whole.shape, jnp.bfloat16),
        ],
        in_specs=[pl.BlockSpec(memory_space=SMEM)] + [near] * 6,
        out_specs=[near, near],
        input_output_aliases={6: 1},
        compiler_params=params(),
        cost_estimate=cost(2),
        name="far",
    )(place, mine, its, before, low, high, whole)


TOP = 32767.0
SHIFT = 16


def encode(blocks):
    lane = lax.broadcasted_iota(jnp.int32, blocks[0].shape, 1)
    largest = jnp.zeros_like(blocks[0])
    for index, block in enumerate(blocks):
        size = jnp.max(jnp.abs(block), axis=1, keepdims=True)
        largest = jnp.where(lane == index, size, largest)
    exponent = jnp.floor(jnp.log2(jnp.maximum(largest, 1e-36)))
    exponent = jnp.clip(exponent, -118.0, 118.0)
    down = jnp.exp2(-exponent)
    mantissa = jnp.maximum(jnp.ceil(largest * down * 64.0), 1.0)
    back = (64.0 * TOP) / mantissa
    codes = []
    for index, block in enumerate(blocks):
        code = (block * down[:, index : index + 1]) * back[:, index : index + 1]
        code = jnp.clip(jnp.round(code), -TOP, TOP)
        codes.append(code.astype(jnp.int32).astype(jnp.int16))
    count = len(blocks)
    beside = jnp.where(lane < count, exponent, 0.0)
    moved = pltpu.roll(mantissa, SHIFT, 1)
    beside = jnp.where((lane >= SHIFT) & (lane < SHIFT + count), moved, beside)
    codes.append(beside.astype(jnp.int32).astype(jnp.int16))
    return codes


def decode_scales(beside):
    value = beside.astype(jnp.int32).astype(jnp.float32)
    lane = lax.broadcasted_iota(jnp.int32, value.shape, 1)
    mantissa = pltpu.roll(value, NB - SHIFT, 1)
    return (mantissa / (64.0 * TOP)) * jnp.exp2(jnp.where(lane < SHIFT, value, 0.0))


def chunk_of(stored):
    return 18 * NB if stored % (18 * NB) == 0 else 9 * NB


def update_kernel(core, shares, factor, chased, panel, panel_other, out, factored):
    @pl.when(pl.program_id(0) == 0)
    def _():
        low, high = shares[0], shares[1]
        for index in range(1, shares.shape[0] // 2):
            low = low + shares[2 * index]
            high = high + shares[2 * index + 1]
        product = lax.dot_general(
            jnp.concatenate([low, high], axis=1),
            factor[...],
            (((1,), (1,)), ((), ())),
            precision=HIGH,
            preferred_element_type=jnp.float32,
        )
        half = product.shape[1] // 2
        turned = jnp.concatenate([product[:, half:], product[:, :half]], axis=1)
        factored[...] = parts_of(jnp.where(core[0] == 0, product, turned), 3)

    term = lax.dot_general(
        factored[...],
        jnp.concatenate([panel[...], panel_other[...]], axis=1),
        (((1,), (1,)), ((), ())),
        preferred_element_type=jnp.float32,
    )
    value = chased[...] - sum_parts(term, 3)
    depth = out.shape[1] - 1
    for where in range(out.shape[0]):
        first = where * depth
        codes = encode(
            [value[:, (first + b) * NB : (first + b + 1) * NB] for b in range(depth)]
        )
        for index, code in enumerate(codes):
            out[where, index] = code


def update(core, shares, factor, chased, panel, panel_other, row_count):
    rows, stored = chased.shape
    half = panel.shape[1]
    chunk = chunk_of(stored)
    depth = stored // (row_count * NB)
    parts = chunk // (depth * NB)
    return pl.pallas_call(
        update_kernel,
        grid=(stored // chunk,),
        out_shape=jax.ShapeDtypeStruct((row_count, depth + 1, rows, NB), jnp.int16),
        in_specs=[
            pl.BlockSpec(memory_space=SMEM),
            pl.BlockSpec(shares.shape, lambda i: (0, 0, 0)),
            pl.BlockSpec(factor.shape, lambda i: (0, 0)),
            pl.BlockSpec((rows, chunk), lambda i: (0, i)),
            pl.BlockSpec((chunk, half), lambda i: (i, 0)),
            pl.BlockSpec((chunk, half), lambda i: (i, 0)),
        ],
        out_specs=pl.BlockSpec((parts, depth + 1, rows, NB), lambda i: (i, 0, 0, 0)),
        scratch_shapes=[pltpu.VMEM((3 * rows, 2 * half), jnp.bfloat16)],
        compiler_params=params("arbitrary"),
        cost_estimate=cost(6),
        name="update",
    )(core, shares, factor, chased, panel, panel_other)


def reorder_kernel(slots, table, isotope, blocks, out, triples, picked):
    sources, rows = blocks.shape[0], blocks.shape[2]
    depth = blocks.shape[1] - 1
    scales = [decode_scales(blocks[source, depth]) for source in range(sources)]

    def block(source, b):
        code = blocks[source, b].astype(jnp.int32).astype(jnp.float32)
        return code * scales[source][:, b : b + 1]

    groups = out.shape[1] // (3 * NB)
    here = lax.broadcasted_iota(jnp.int32, (3 * NB, 3 * NB), 0)
    there = lax.broadcasted_iota(jnp.int32, (3 * NB, 3 * NB), 1)
    spread = (here == 3 * (there % NB) + there // NB).astype(jnp.bfloat16)
    closed = (there == 3 * (here % NB) + here // NB).astype(jnp.bfloat16)

    kind = isotope[...]
    mass = jnp.full(kind.shape, 1.0, jnp.float32)
    for index in range(table.shape[0]):
        mass = jnp.where(kind == index, table[index], mass)
    scale = 1.0 / jnp.sqrt(mass)

    per = sources // 3
    for group in range(groups):
        b, q = group // per, group % per
        wide = jnp.concatenate([block(3 * q + k, b) for k in range(3)], axis=1)
        apart = sum_parts(
            jnp.dot(parts_of(wide, 2), spread, preferred_element_type=jnp.float32), 2
        )
        tall = jnp.concatenate(
            [apart[:, c * NB : (c + 1) * NB] for c in range(3)]
            + [jnp.zeros((NB - 3 * rows, NB), jnp.float32)],
            axis=0,
        )
        triples[group * NB : (group + 1) * NB, :] = tall.T

    unroll = 32

    def pick(step, carry):
        start = pl.multiple_of(step * unroll, unroll)
        for index in range(unroll):
            slot = slots[0, start + index]
            picked[pl.ds(start + index, 1), :] = triples[pl.ds(slot, 1), :]
        return carry

    lax.fori_loop(0, slots.shape[1] // unroll, pick, 0)

    for group in range(groups):
        tall = picked[group * NB : (group + 1) * NB, :].T
        factor = scale[group : group + 1, :]
        wide = jnp.concatenate(
            [tall[c * rows : (c + 1) * rows] * factor for c in range(3)], axis=1
        )
        out[:, group * 3 * NB : (group + 1) * 3 * NB] = sum_parts(
            jnp.dot(parts_of(wide, 2), closed, preferred_element_type=jnp.float32), 2
        )


def reorder(blocks, slots, isotope, table):
    sources, rows = blocks.shape[0], blocks.shape[2]
    stored = sources * (blocks.shape[1] - 1) * NB
    atoms = stored // 3
    return pl.pallas_call(
        reorder_kernel,
        out_shape=jax.ShapeDtypeStruct((rows, stored), jnp.float32),
        in_specs=[
            pl.BlockSpec(memory_space=SMEM),
            pl.BlockSpec(memory_space=SMEM),
            pl.BlockSpec(memory_space=VMEM),
            pl.BlockSpec(memory_space=VMEM),
        ],
        out_specs=pl.BlockSpec(memory_space=VMEM),
        scratch_shapes=[
            pltpu.VMEM((atoms, NB), jnp.float32),
            pltpu.VMEM((atoms, NB), jnp.float32),
        ],
        compiler_params=params(),
        cost_estimate=cost(10),
        name="reorder",
    )(slots, table, isotope.reshape(-1, NB), blocks)


ROW = ("x", "z_lo")
COL = ("y", "z_hi", "core")
SIZES = (4, 3, 8, 4, 2)


def exchange(value, axes):
    return lax.all_to_all(value, axes, split_axis=0, concat_axis=0, tiled=True)


def other_core(value):
    return lax.ppermute(value, "core", [(0, 1), (1, 0)])


def shift(value, by):
    size = lax.axis_size("y")
    return lax.ppermute(value, "y", [(i, (i + by) % size) for i in range(size)])


def gather_half(panel):
    half = panel.shape[1] // 2
    first = lax.axis_index("core") == 0
    low, high = panel[:, :half], panel[:, half:]
    kept = jnp.where(first, low, high)
    got = other_core(jnp.where(first, high, low))
    pair = jnp.concatenate([jnp.where(first, kept, got), jnp.where(first, got, kept)])
    plane = lax.all_gather(pair, "z_hi", axis=0)
    up = down = plane
    pieces, steps = [plane], [0]
    for step in range(1, lax.axis_size("y") // 2):
        up, down = shift(up, 1), shift(down, -1)
        pieces += [up, down]
        steps += [-step, step]
    cut = plane.shape[0] // 2
    return pieces, steps, shift(up[:cut], 1), shift(down[cut:], -1)


def per_device(
    band_vectors,
    bulge_vectors,
    counts,
    offsets,
    panel_vectors,
    factor,
    atom_slot,
    isotope,
    mass_table,
):
    row_count = lax.axis_size(ROW)
    core = lax.axis_index("core").astype(jnp.int32)
    place = jnp.stack([core, lax.axis_index("y").astype(jnp.int32)])
    pieces, steps, low, high = gather_half(panel_vectors)
    chased, mine = chase(
        band_vectors, bulge_vectors[0], counts, offsets, lax.axis_size("y")
    )
    its = other_core(mine)
    before, whole = project_near(place, mine, its, pieces, steps)
    sums, panel = project_far(place, mine, its, before, low, high, whole, row_count)
    panel_other = other_core(panel)
    panel = panel.reshape(-1, panel.shape[3])
    panel_other = panel_other.reshape(panel.shape)
    shares = exchange(sums, ROW + ("core",))
    updated = update(place, shares, factor, chased, panel, panel_other, row_count)
    moved = exchange(updated, ROW)
    return reorder(moved, atom_slot, isotope, mass_table)


def solution(mesh):
    fine = Mesh(mesh.devices.reshape(SIZES), ROW + COL)
    in_specs = (
        P(COL, ROW),
        P(ROW, None, None),
        P(ROW),
        P(ROW, None),
        P(ROW + COL, None),
        P(),
        P(ROW, None),
        P(ROW),
        P(),
    )
    return jax.shard_map(
        per_device,
        mesh=fine,
        in_specs=in_specs,
        out_specs=P(COL, ROW),
        check_vma=False,
    )
```

```python
import functools

import jax
import jax.numpy as jnp
from jax import lax
from jax.experimental import pallas as pl
from jax.experimental.pallas import tpu as pltpu
from jax.sharding import Mesh
from jax.sharding import PartitionSpec as P

NB = 128
HIGH = lax.Precision.HIGHEST
VMEM = pltpu.VMEM
SMEM = pltpu.SMEM
LIMIT = 16 * 1024 * 1024


def cost(microseconds):
    return pl.CostEstimate(
        flops=0, bytes_accessed=int(3.0e6 * microseconds), transcendentals=0
    )


def params(*semantics):
    return pltpu.CompilerParams(
        vmem_limit_bytes=LIMIT, dimension_semantics=semantics or None
    )


def parts_of(value, amount):
    parts = []
    for _ in range(amount):
        part = value.astype(jnp.bfloat16)
        parts.append(part)
        value = value - part.astype(jnp.float32)
    return jnp.concatenate(parts, axis=0)


def sum_parts(value, amount):
    rows = value.shape[0] // amount
    total = value[(amount - 1) * rows :]
    for index in reversed(range(amount - 1)):
        total = total + value[index * rows : (index + 1) * rows]
    return total


def chase_kernel(counts, offsets, band, vectors, out, places):
    slots, width = vectors.shape
    stored = band.shape[1]
    span = 2 * width
    low = offsets[0, 0]
    for slot in range(1, slots):
        low = jnp.minimum(low, offsets[0, slot])
    base = jnp.minimum((low // NB) * NB, stored - span)
    base = pl.multiple_of(base, NB)
    out[...] = band[...]
    window = band[:, pl.ds(base, span)]
    every = vectors[...]
    scaling = 2.0 / (jnp.sum(every * every, axis=1, keepdims=True) + 1e-06)
    for slot in range(slots):
        row = jnp.concatenate(
            [every[slot : slot + 1], jnp.zeros((1, span - width), jnp.float32)], axis=1
        )
        row = jnp.broadcast_to(row, (8, span))
        row = pltpu.roll(row, offsets[0, slot] - base, 1)
        row = jnp.concatenate([row] * (band.shape[0] // 8), axis=0)
        inner = jnp.sum(window * row, axis=1, keepdims=True)
        factor = jnp.where(slot < counts[0], scaling[slot : slot + 1], 0.0)
        window = window - (factor * inner) * row
    out[:, pl.ds(base, span)] = window
    part = places.shape[2]
    for index in range(places.shape[0]):
        places[index] = out[:, index * part : (index + 1) * part]


def chase(band, vectors, counts, offsets, places):
    rows, stored = band.shape
    return pl.pallas_call(
        chase_kernel,
        out_shape=[
            jax.ShapeDtypeStruct(band.shape, jnp.float32),
            jax.ShapeDtypeStruct((places, rows, stored // places), jnp.float32),
        ],
        in_specs=[
            pl.BlockSpec(memory_space=SMEM),
            pl.BlockSpec(memory_space=SMEM),
            pl.BlockSpec(memory_space=VMEM),
            pl.BlockSpec(memory_space=VMEM),
        ],
        out_specs=[pl.BlockSpec(memory_space=VMEM)] * 2,
        compiler_params=params(),
        cost_estimate=cost(4),
        name="chase",
    )(counts, offsets, band, vectors)


def place_product(mine, its, source, part):
    both = jnp.concatenate([mine[source], its[source]], axis=0)
    flat = part.reshape(part.shape[0] * part.shape[1], part.shape[2])
    return jnp.dot(parts_of(both, 3), flat, preferred_element_type=jnp.float32)


def near_kernel(place, mine, its, *rest, steps):
    pieces, (out, whole) = rest[: len(steps)], rest[len(steps) :]
    count = whole.shape[0]
    done = jnp.zeros((3 * out.shape[0], out.shape[1]), jnp.float32)
    for piece, step in zip(pieces, steps):
        source = lax.rem(place[1] + step + count, count)
        part = piece[...]
        whole[source] = part
        done = done + place_product(mine, its, source, part)
    out[...] = sum_parts(done, 3)


def project_near(place, mine, its, pieces, steps):
    count, rows, _ = mine.shape
    shape = pieces[0].shape
    near = pl.BlockSpec(memory_space=VMEM)
    return pl.pallas_call(
        functools.partial(near_kernel, steps=steps),
        out_shape=[
            jax.ShapeDtypeStruct((2 * rows, shape[2]), jnp.float32),
            jax.ShapeDtypeStruct((count,) + shape, jnp.bfloat16),
        ],
        in_specs=[pl.BlockSpec(memory_space=SMEM)] + [near] * (2 + len(pieces)),
        out_specs=[near, near],
        compiler_params=params(),
        cost_estimate=cost(6),
        name="near",
    )(place, mine, its, *pieces)


def far_kernel(place, mine, its, before, low, high, _, out, whole):
    count = whole.shape[0]
    rows = before.shape[0] // 2
    source = lax.rem(place[1] + count // 2, count)
    part = jnp.concatenate([low[...], high[...]], axis=0)
    whole[source] = part
    product = place_product(mine, its, source, part)
    done = before[...] + sum_parts(product, 3)
    zero = place[0] == 0
    own, other = done[:rows], done[rows:]
    even, odd = jnp.where(zero, own, other), jnp.where(zero, other, own)
    for index in range(out.shape[0] // 2):
        out[2 * index] = even
        out[2 * index + 1] = odd


def project_far(place, mine, its, before, low, high, whole, copies):
    rows = mine.shape[1]
    near = pl.BlockSpec(memory_space=VMEM)
    return pl.pallas_call(
        far_kernel,
        out_shape=[
            jax.ShapeDtypeStruct((2 * copies, rows, whole.shape[3]), jnp.float32),
            jax.ShapeDtypeStruct(whole.shape, jnp.bfloat16),
        ],
        in_specs=[pl.BlockSpec(memory_space=SMEM)] + [near] * 6,
        out_specs=[near, near],
        input_output_aliases={6: 1},
        compiler_params=params(),
        cost_estimate=cost(2),
        name="far",
    )(place, mine, its, before, low, high, whole)


TOP = 32767.0
SHIFT = 16


def encode(blocks):
    lane = lax.broadcasted_iota(jnp.int32, blocks[0].shape, 1)
    largest = jnp.zeros_like(blocks[0])
    for index, block in enumerate(blocks):
        size = jnp.max(jnp.abs(block), axis=1, keepdims=True)
        largest = jnp.where(lane == index, size, largest)
    exponent = jnp.floor(jnp.log2(jnp.maximum(largest, 1e-36)))
    exponent = jnp.clip(exponent, -118.0, 118.0)
    down = jnp.exp2(-exponent)
    mantissa = jnp.maximum(jnp.ceil(largest * down * 64.0), 1.0)
    back = (64.0 * TOP) / mantissa
    codes = []
    for index, block in enumerate(blocks):
        code = (block * down[:, index : index + 1]) * back[:, index : index + 1]
        code = jnp.clip(jnp.round(code), -TOP, TOP)
        codes.append(code.astype(jnp.int32).astype(jnp.int16))
    count = len(blocks)
    beside = jnp.where(lane < count, exponent, 0.0)
    moved = pltpu.roll(mantissa, SHIFT, 1)
    beside = jnp.where((lane >= SHIFT) & (lane < SHIFT + count), moved, beside)
    codes.append(beside.astype(jnp.int32).astype(jnp.int16))
    return codes


def decode_scales(beside):
    value = beside.astype(jnp.int32).astype(jnp.float32)
    lane = lax.broadcasted_iota(jnp.int32, value.shape, 1)
    mantissa = pltpu.roll(value, NB - SHIFT, 1)
    return (mantissa / (64.0 * TOP)) * jnp.exp2(jnp.where(lane < SHIFT, value, 0.0))


def chunk_of(stored):
    return 18 * NB if stored % (18 * NB) == 0 else 9 * NB


def update_kernel(core, shares, factor, chased, panel, panel_other, out, factored):
    @pl.when(pl.program_id(0) == 0)
    def _():
        low, high = shares[0], shares[1]
        for index in range(1, shares.shape[0] // 2):
            low = low + shares[2 * index]
            high = high + shares[2 * index + 1]
        product = lax.dot_general(
            jnp.concatenate([low, high], axis=1),
            factor[...],
            (((1,), (1,)), ((), ())),
            precision=HIGH,
            preferred_element_type=jnp.float32,
        )
        half = product.shape[1] // 2
        turned = jnp.concatenate([product[:, half:], product[:, :half]], axis=1)
        factored[...] = parts_of(jnp.where(core[0] == 0, product, turned), 3)

    term = lax.dot_general(
        factored[...],
        jnp.concatenate([panel[...], panel_other[...]], axis=1),
        (((1,), (1,)), ((), ())),
        preferred_element_type=jnp.float32,
    )
    value = chased[...] - sum_parts(term, 3)
    depth = out.shape[1] - 1
    for where in range(out.shape[0]):
        first = where * depth
        codes = encode(
            [value[:, (first + b) * NB : (first + b + 1) * NB] for b in range(depth)]
        )
        for index, code in enumerate(codes):
            out[where, index] = code


def update(core, shares, factor, chased, panel, panel_other, row_count):
    rows, stored = chased.shape
    half = panel.shape[1]
    chunk = chunk_of(stored)
    depth = stored // (row_count * NB)
    parts = chunk // (depth * NB)
    return pl.pallas_call(
        update_kernel,
        grid=(stored // chunk,),
        out_shape=jax.ShapeDtypeStruct((row_count, depth + 1, rows, NB), jnp.int16),
        in_specs=[
            pl.BlockSpec(memory_space=SMEM),
            pl.BlockSpec(shares.shape, lambda i: (0, 0, 0)),
            pl.BlockSpec(factor.shape, lambda i: (0, 0)),
            pl.BlockSpec((rows, chunk), lambda i: (0, i)),
            pl.BlockSpec((chunk, half), lambda i: (i, 0)),
            pl.BlockSpec((chunk, half), lambda i: (i, 0)),
        ],
        out_specs=pl.BlockSpec((parts, depth + 1, rows, NB), lambda i: (i, 0, 0, 0)),
        scratch_shapes=[pltpu.VMEM((3 * rows, 2 * half), jnp.bfloat16)],
        compiler_params=params("arbitrary"),
        cost_estimate=cost(6),
        name="update",
    )(core, shares, factor, chased, panel, panel_other)


def reorder_kernel(slots, table, isotope, blocks, out, triples, picked, staged, turned):
    sources, rows = blocks.shape[0], blocks.shape[2]
    depth = blocks.shape[1] - 1
    scales = [decode_scales(blocks[source, depth]) for source in range(sources)]

    def block(source, b):
        code = blocks[source, b].astype(jnp.int32).astype(jnp.float32)
        return code * scales[source][:, b : b + 1]

    groups = out.shape[1] // (3 * NB)
    here = lax.broadcasted_iota(jnp.int32, (3 * NB, 3 * NB), 0)
    there = lax.broadcasted_iota(jnp.int32, (3 * NB, 3 * NB), 1)
    spread = (here == 3 * (there % NB) + there // NB).astype(jnp.bfloat16)
    closed = (there == 3 * (here % NB) + here // NB).astype(jnp.bfloat16)

    kind = isotope[...]
    mass = jnp.full(kind.shape, 1.0, jnp.float32)
    for index in range(table.shape[0]):
        mass = jnp.where(kind == index, table[index], mass)
    scale = 1.0 / jnp.sqrt(mass)

    per = sources // 3
    tall_rows = 2 * rows
    for group in range(groups):
        b, q = group // per, group % per
        wide = jnp.concatenate([block(3 * q + k, b) for k in range(3)], axis=1)
        staged[group * tall_rows : (group + 1) * tall_rows, :] = parts_of(wide, 2)
    turned[...] = jnp.dot(staged[...], spread, preferred_element_type=jnp.float32)
    for group in range(groups):
        apart = sum_parts(turned[group * tall_rows : (group + 1) * tall_rows, :], 2)
        tall = jnp.concatenate(
            [apart[:, c * NB : (c + 1) * NB] for c in range(3)]
            + [jnp.zeros((NB - 3 * rows, NB), jnp.float32)],
            axis=0,
        )
        triples[group * NB : (group + 1) * NB, :] = tall.T

    unroll = 64

    def pick(step, carry):
        start = pl.multiple_of(step * unroll, unroll)
        for index in range(unroll):
            slot = slots[0, start + index]
            picked[pl.ds(start + index, 1), :] = triples[pl.ds(slot, 1), :]
        return carry

    lax.fori_loop(0, slots.shape[1] // unroll, pick, 0)

    for group in range(groups):
        tall = picked[group * NB : (group + 1) * NB, :].T
        factor = scale[group : group + 1, :]
        wide = jnp.concatenate(
            [tall[c * rows : (c + 1) * rows] * factor for c in range(3)], axis=1
        )
        staged[group * tall_rows : (group + 1) * tall_rows, :] = parts_of(wide, 2)
    turned[...] = jnp.dot(staged[...], closed, preferred_element_type=jnp.float32)
    for group in range(groups):
        out[:, group * 3 * NB : (group + 1) * 3 * NB] = sum_parts(
            turned[group * tall_rows : (group + 1) * tall_rows, :], 2
        )


def reorder(blocks, slots, isotope, table):
    sources, rows = blocks.shape[0], blocks.shape[2]
    stored = sources * (blocks.shape[1] - 1) * NB
    atoms = stored // 3
    return pl.pallas_call(
        reorder_kernel,
        out_shape=jax.ShapeDtypeStruct((rows, stored), jnp.float32),
        in_specs=[
            pl.BlockSpec(memory_space=SMEM),
            pl.BlockSpec(memory_space=SMEM),
            pl.BlockSpec(memory_space=VMEM),
            pl.BlockSpec(memory_space=VMEM),
        ],
        out_specs=pl.BlockSpec(memory_space=VMEM),
        scratch_shapes=[
            pltpu.VMEM((atoms, NB), jnp.float32),
            pltpu.VMEM((atoms, NB), jnp.float32),
            pltpu.VMEM((2 * rows * atoms // NB, 3 * NB), jnp.bfloat16),
            pltpu.VMEM((2 * rows * atoms // NB, 3 * NB), jnp.float32),
        ],
        compiler_params=params(),
        cost_estimate=cost(10),
        name="reorder",
    )(slots, table, isotope.reshape(-1, NB), blocks)


ROW = ("x", "z_lo")
COL = ("y", "z_hi", "core")
SIZES = (4, 3, 8, 4, 2)


def exchange(value, axes):
    return lax.all_to_all(value, axes, split_axis=0, concat_axis=0, tiled=True)


def other_core(value):
    return lax.ppermute(value, "core", [(0, 1), (1, 0)])


def shift(value, by):
    size = lax.axis_size("y")
    return lax.ppermute(value, "y", [(i, (i + by) % size) for i in range(size)])


def gather_half(panel):
    half = panel.shape[1] // 2
    first = lax.axis_index("core") == 0
    got = other_core(panel)
    pair = jnp.where(
        first,
        jnp.concatenate([panel[:, :half], got[:, :half]]),
        jnp.concatenate([got[:, half:], panel[:, half:]]),
    )
    plane = lax.all_gather(pair, "z_hi", axis=0)
    up = down = plane
    pieces, steps = [plane], [0]
    for step in range(1, lax.axis_size("y") // 2):
        up, down = shift(up, 1), shift(down, -1)
        pieces += [up, down]
        steps += [-step, step]
    cut = plane.shape[0] // 2
    return pieces, steps, shift(up[:cut], 1), shift(down[cut:], -1)


def per_device(
    band_vectors,
    bulge_vectors,
    counts,
    offsets,
    panel_vectors,
    factor,
    atom_slot,
    isotope,
    mass_table,
):
    row_count = lax.axis_size(ROW)
    core = lax.axis_index("core").astype(jnp.int32)
    place = jnp.stack([core, lax.axis_index("y").astype(jnp.int32)])
    pieces, steps, low, high = gather_half(panel_vectors)
    chased, mine = chase(
        band_vectors, bulge_vectors[0], counts, offsets, lax.axis_size("y")
    )
    its = other_core(mine)
    before, whole = project_near(place, mine, its, pieces, steps)
    sums, panel = project_far(place, mine, its, before, low, high, whole, row_count)
    panel_other = other_core(panel)
    panel = panel.reshape(-1, panel.shape[3])
    panel_other = panel_other.reshape(panel.shape)
    shares = exchange(sums, ROW + ("core",))
    updated = update(place, shares, factor, chased, panel, panel_other, row_count)
    moved = exchange(updated, ROW)
    return reorder(moved, atom_slot, isotope, mass_table)


def solution(mesh):
    fine = Mesh(mesh.devices.reshape(SIZES), ROW + COL)
    in_specs = (
        P(COL, ROW),
        P(ROW, None, None),
        P(ROW),
        P(ROW, None),
        P(ROW + COL, None),
        P(),
        P(ROW, None),
        P(ROW),
        P(),
    )
    return jax.shard_map(
        per_device,
        mesh=fine,
        in_specs=in_specs,
        out_specs=P(COL, ROW),
        check_vma=False,
    )
```

```python
import functools

import jax
import jax.numpy as jnp
from jax import lax
from jax.experimental import pallas as pl
from jax.experimental.pallas import tpu as pltpu
from jax.sharding import Mesh
from jax.sharding import PartitionSpec as P

NB = 128
HIGH = lax.Precision.HIGHEST
VMEM = pltpu.VMEM
SMEM = pltpu.SMEM
LIMIT = 16 * 1024 * 1024


def cost(microseconds):
    return pl.CostEstimate(
        flops=0, bytes_accessed=int(3.0e6 * microseconds), transcendentals=0
    )


def params(*semantics):
    return pltpu.CompilerParams(
        vmem_limit_bytes=LIMIT, dimension_semantics=semantics or None
    )


def parts_of(value, amount):
    parts = []
    for _ in range(amount):
        part = value.astype(jnp.bfloat16)
        parts.append(part)
        value = value - part.astype(jnp.float32)
    return jnp.concatenate(parts, axis=0)


def sum_parts(value, amount):
    rows = value.shape[0] // amount
    total = value[(amount - 1) * rows :]
    for index in reversed(range(amount - 1)):
        total = total + value[index * rows : (index + 1) * rows]
    return total


def chase_kernel(counts, offsets, band, vectors, out, places):
    slots, width = vectors.shape
    stored = band.shape[1]
    span = 2 * width
    low = offsets[0, 0]
    for slot in range(1, slots):
        low = jnp.minimum(low, offsets[0, slot])
    base = jnp.minimum((low // NB) * NB, stored - span)
    base = pl.multiple_of(base, NB)
    out[...] = band[...]
    window = band[:, pl.ds(base, span)]
    every = vectors[...]
    scaling = 2.0 / (jnp.sum(every * every, axis=1, keepdims=True) + 1e-06)
    for slot in range(slots):
        row = jnp.concatenate(
            [every[slot : slot + 1], jnp.zeros((1, span - width), jnp.float32)], axis=1
        )
        row = jnp.broadcast_to(row, (8, span))
        row = pltpu.roll(row, offsets[0, slot] - base, 1)
        row = jnp.concatenate([row] * (band.shape[0] // 8), axis=0)
        inner = jnp.sum(window * row, axis=1, keepdims=True)
        factor = jnp.where(slot < counts[0], scaling[slot : slot + 1], 0.0)
        window = window - (factor * inner) * row
    out[:, pl.ds(base, span)] = window
    part = places.shape[2]
    for index in range(places.shape[0]):
        places[index] = out[:, index * part : (index + 1) * part]


def chase(band, vectors, counts, offsets, places):
    rows, stored = band.shape
    return pl.pallas_call(
        chase_kernel,
        out_shape=[
            jax.ShapeDtypeStruct(band.shape, jnp.float32),
            jax.ShapeDtypeStruct((places, rows, stored // places), jnp.float32),
        ],
        in_specs=[
            pl.BlockSpec(memory_space=SMEM),
            pl.BlockSpec(memory_space=SMEM),
            pl.BlockSpec(memory_space=VMEM),
            pl.BlockSpec(memory_space=VMEM),
        ],
        out_specs=[pl.BlockSpec(memory_space=VMEM)] * 2,
        compiler_params=params(),
        cost_estimate=cost(4),
        name="chase",
    )(counts, offsets, band, vectors)


def place_product(mine, its, source, part):
    both = jnp.concatenate([mine[source], its[source]], axis=0)
    flat = part.reshape(part.shape[0] * part.shape[1], part.shape[2])
    return jnp.dot(parts_of(both, 3), flat, preferred_element_type=jnp.float32)


def near_kernel(place, mine, its, *rest, steps):
    pieces, (out, whole) = rest[: len(steps)], rest[len(steps) :]
    count = whole.shape[0]
    done = jnp.zeros((3 * out.shape[0], out.shape[1]), jnp.float32)
    for piece, step in zip(pieces, steps):
        source = lax.rem(place[1] + step + count, count)
        part = piece[...]
        whole[source] = part
        done = done + place_product(mine, its, source, part)
    out[...] = sum_parts(done, 3)


def project_near(place, mine, its, pieces, steps):
    count, rows, _ = mine.shape
    shape = pieces[0].shape
    near = pl.BlockSpec(memory_space=VMEM)
    return pl.pallas_call(
        functools.partial(near_kernel, steps=steps),
        out_shape=[
            jax.ShapeDtypeStruct((2 * rows, shape[2]), jnp.float32),
            jax.ShapeDtypeStruct((count,) + shape, jnp.bfloat16),
        ],
        in_specs=[pl.BlockSpec(memory_space=SMEM)] + [near] * (2 + len(pieces)),
        out_specs=[near, near],
        compiler_params=params(),
        cost_estimate=cost(6),
        name="near",
    )(place, mine, its, *pieces)


def far_kernel(place, mine, its, before, low, high, _, out, whole):
    count = whole.shape[0]
    rows = before.shape[0] // 2
    source = lax.rem(place[1] + count // 2, count)
    part = jnp.concatenate([low[...], high[...]], axis=0)
    whole[source] = part
    product = place_product(mine, its, source, part)
    done = before[...] + sum_parts(product, 3)
    zero = place[0] == 0
    own, other = done[:rows], done[rows:]
    even, odd = jnp.where(zero, own, other), jnp.where(zero, other, own)
    for index in range(out.shape[0] // 2):
        out[2 * index] = even
        out[2 * index + 1] = odd


def project_far(place, mine, its, before, low, high, whole, copies):
    rows = mine.shape[1]
    near = pl.BlockSpec(memory_space=VMEM)
    return pl.pallas_call(
        far_kernel,
        out_shape=[
            jax.ShapeDtypeStruct((2 * copies, rows, whole.shape[3]), jnp.float32),
            jax.ShapeDtypeStruct(whole.shape, jnp.bfloat16),
        ],
        in_specs=[pl.BlockSpec(memory_space=SMEM)] + [near] * 6,
        out_specs=[near, near],
        input_output_aliases={6: 1},
        compiler_params=params(),
        cost_estimate=cost(2),
        name="far",
    )(place, mine, its, before, low, high, whole)


TOP = 32767.0
SHIFT = 16


def encode(blocks):
    lane = lax.broadcasted_iota(jnp.int32, blocks[0].shape, 1)
    largest = jnp.zeros_like(blocks[0])
    for index, block in enumerate(blocks):
        size = jnp.max(jnp.abs(block), axis=1, keepdims=True)
        largest = jnp.where(lane == index, size, largest)
    exponent = jnp.floor(jnp.log2(jnp.maximum(largest, 1e-36)))
    exponent = jnp.clip(exponent, -118.0, 118.0)
    down = jnp.exp2(-exponent)
    mantissa = jnp.maximum(jnp.ceil(largest * down * 64.0), 1.0)
    back = (64.0 * TOP) / mantissa
    codes = []
    for index, block in enumerate(blocks):
        code = (block * down[:, index : index + 1]) * back[:, index : index + 1]
        code = jnp.clip(jnp.round(code), -TOP, TOP)
        codes.append(code.astype(jnp.int32).astype(jnp.int16))
    count = len(blocks)
    beside = jnp.where(lane < count, exponent, 0.0)
    moved = pltpu.roll(mantissa, SHIFT, 1)
    beside = jnp.where((lane >= SHIFT) & (lane < SHIFT + count), moved, beside)
    codes.append(beside.astype(jnp.int32).astype(jnp.int16))
    return codes


def decode_scales(beside):
    value = beside.astype(jnp.int32).astype(jnp.float32)
    lane = lax.broadcasted_iota(jnp.int32, value.shape, 1)
    mantissa = pltpu.roll(value, NB - SHIFT, 1)
    return (mantissa / (64.0 * TOP)) * jnp.exp2(jnp.where(lane < SHIFT, value, 0.0))


def update_kernel(
    core, shares, factor, chased, panel, panel_other, out
):
    low, high = shares[0], shares[1]
    for index in range(1, shares.shape[0] // 2):
        low = low + shares[2 * index]
        high = high + shares[2 * index + 1]
    product = lax.dot_general(
        jnp.concatenate([low, high], axis=1),
        factor[...],
        (((1,), (1,)), ((), ())),
        precision=HIGH,
        preferred_element_type=jnp.float32,
    )
    half = product.shape[1] // 2
    turned = jnp.concatenate([product[:, half:], product[:, :half]], axis=1)
    factored = parts_of(jnp.where(core[0] == 0, product, turned), 3)

    depth = out.shape[1] - 1
    chunk = depth * NB
    for index in range(out.shape[0]):
        lanes = pl.ds(index * chunk, chunk)
        both = jnp.concatenate([panel[lanes], panel_other[lanes]], axis=1)
        term = lax.dot_general(
            factored,
            both,
            (((1,), (1,)), ((), ())),
            preferred_element_type=jnp.float32,
        )
        value = chased[:, lanes] - sum_parts(term, 3)
        codes = encode([value[:, b * NB : (b + 1) * NB] for b in range(depth)])
        for b, code in enumerate(codes):
            out[index, b] = code


def update(core, shares, factor, chased, panel, panel_other, row_count):
    rows, stored = chased.shape
    depth = stored // (row_count * NB)
    near = pl.BlockSpec(memory_space=VMEM)
    return pl.pallas_call(
        update_kernel,
        out_shape=jax.ShapeDtypeStruct((row_count, depth + 1, rows, NB), jnp.int16),
        in_specs=[pl.BlockSpec(memory_space=SMEM)] + [near] * 5,
        out_specs=near,
        compiler_params=params(),
        cost_estimate=cost(6),
        name="update",
    )(core, shares, factor, chased, panel, panel_other)


def reorder_kernel(slots, table, isotope, blocks, out, triples, picked, staged, turned):
    sources, rows = blocks.shape[0], blocks.shape[2]
    depth = blocks.shape[1] - 1
    scales = [decode_scales(blocks[source, depth]) for source in range(sources)]

    def block(source, b):
        code = blocks[source, b].astype(jnp.int32).astype(jnp.float32)
        return code * scales[source][:, b : b + 1]

    groups = out.shape[1] // (3 * NB)
    here = lax.broadcasted_iota(jnp.int32, (3 * NB, 3 * NB), 0)
    there = lax.broadcasted_iota(jnp.int32, (3 * NB, 3 * NB), 1)
    spread = (here == 3 * (there % NB) + there // NB).astype(jnp.bfloat16)
    closed = (there == 3 * (here % NB) + here // NB).astype(jnp.bfloat16)

    kind = isotope[...]
    mass = jnp.full(kind.shape, 1.0, jnp.float32)
    for index in range(table.shape[0]):
        mass = jnp.where(kind == index, table[index], mass)
    scale = 1.0 / jnp.sqrt(mass)

    per = sources // 3
    tall_rows = 2 * rows
    for group in range(groups):
        b, q = group // per, group % per
        wide = jnp.concatenate([block(3 * q + k, b) for k in range(3)], axis=1)
        staged[group * tall_rows : (group + 1) * tall_rows, :] = parts_of(wide, 2)
    turned[...] = jnp.dot(staged[...], spread, preferred_element_type=jnp.float32)
    for group in range(groups):
        apart = sum_parts(turned[group * tall_rows : (group + 1) * tall_rows, :], 2)
        tall = jnp.concatenate(
            [apart[:, c * NB : (c + 1) * NB] for c in range(3)]
            + [jnp.zeros((NB - 3 * rows, NB), jnp.float32)],
            axis=0,
        )
        triples[group * NB : (group + 1) * NB, :] = tall.T

    unroll = 64

    def pick(step, carry):
        start = pl.multiple_of(step * unroll, unroll)
        for index in range(unroll):
            slot = slots[0, start + index]
            picked[pl.ds(start + index, 1), :] = triples[pl.ds(slot, 1), :]
        return carry

    lax.fori_loop(0, slots.shape[1] // unroll, pick, 0)

    for group in range(groups):
        tall = picked[group * NB : (group + 1) * NB, :].T
        factor = scale[group : group + 1, :]
        wide = jnp.concatenate(
            [tall[c * rows : (c + 1) * rows] * factor for c in range(3)], axis=1
        )
        staged[group * tall_rows : (group + 1) * tall_rows, :] = parts_of(wide, 2)
    turned[...] = jnp.dot(staged[...], closed, preferred_element_type=jnp.float32)
    for group in range(groups):
        out[:, group * 3 * NB : (group + 1) * 3 * NB] = sum_parts(
            turned[group * tall_rows : (group + 1) * tall_rows, :], 2
        )


def reorder(blocks, slots, isotope, table):
    sources, rows = blocks.shape[0], blocks.shape[2]
    stored = sources * (blocks.shape[1] - 1) * NB
    atoms = stored // 3
    return pl.pallas_call(
        reorder_kernel,
        out_shape=jax.ShapeDtypeStruct((rows, stored), jnp.float32),
        in_specs=[
            pl.BlockSpec(memory_space=SMEM),
            pl.BlockSpec(memory_space=SMEM),
            pl.BlockSpec(memory_space=VMEM),
            pl.BlockSpec(memory_space=VMEM),
        ],
        out_specs=pl.BlockSpec(memory_space=VMEM),
        scratch_shapes=[
            pltpu.VMEM((atoms, NB), jnp.float32),
            pltpu.VMEM((atoms, NB), jnp.float32),
            pltpu.VMEM((2 * rows * atoms // NB, 3 * NB), jnp.bfloat16),
            pltpu.VMEM((2 * rows * atoms // NB, 3 * NB), jnp.float32),
        ],
        compiler_params=params(),
        cost_estimate=cost(10),
        name="reorder",
    )(slots, table, isotope.reshape(-1, NB), blocks)


ROW = ("x", "z_lo")
COL = ("y", "z_hi", "core")
SIZES = (4, 3, 8, 4, 2)


def exchange(value, axes):
    return lax.all_to_all(value, axes, split_axis=0, concat_axis=0, tiled=True)


def other_core(value):
    return lax.ppermute(value, "core", [(0, 1), (1, 0)])


def shift(value, by):
    size = lax.axis_size("y")
    return lax.ppermute(value, "y", [(i, (i + by) % size) for i in range(size)])


def gather_half(panel):
    half = panel.shape[1] // 2
    first = lax.axis_index("core") == 0
    got = other_core(panel)
    pair = jnp.where(
        first,
        jnp.concatenate([panel[:, :half], got[:, :half]]),
        jnp.concatenate([got[:, half:], panel[:, half:]]),
    )
    plane = lax.all_gather(pair, "z_hi", axis=0)
    up = down = plane
    pieces, steps = [plane], [0]
    for step in range(1, lax.axis_size("y") // 2):
        up, down = shift(up, 1), shift(down, -1)
        pieces += [up, down]
        steps += [-step, step]
    cut = plane.shape[0] // 2
    return pieces, steps, shift(up[:cut], 1), shift(down[cut:], -1)


def per_device(
    band_vectors,
    bulge_vectors,
    counts,
    offsets,
    panel_vectors,
    factor,
    atom_slot,
    isotope,
    mass_table,
):
    row_count = lax.axis_size(ROW)
    core = lax.axis_index("core").astype(jnp.int32)
    place = jnp.stack([core, lax.axis_index("y").astype(jnp.int32)])
    pieces, steps, low, high = gather_half(panel_vectors)
    chased, mine = chase(
        band_vectors, bulge_vectors[0], counts, offsets, lax.axis_size("y")
    )
    its = other_core(mine)
    before, whole = project_near(place, mine, its, pieces, steps)
    sums, panel = project_far(place, mine, its, before, low, high, whole, row_count)
    panel_other = other_core(panel)
    panel = panel.reshape(-1, panel.shape[3])
    panel_other = panel_other.reshape(panel.shape)
    shares = exchange(sums, ROW + ("core",))
    updated = update(place, shares, factor, chased, panel, panel_other, row_count)
    moved = exchange(updated, ROW)
    return reorder(moved, atom_slot, isotope, mass_table)


def solution(mesh):
    fine = Mesh(mesh.devices.reshape(SIZES), ROW + COL)
    in_specs = (
        P(COL, ROW),
        P(ROW, None, None),
        P(ROW),
        P(ROW, None),
        P(ROW + COL, None),
        P(),
        P(ROW, None),
        P(ROW),
        P(),
    )
    return jax.shard_map(
        per_device,
        mesh=fine,
        in_specs=in_specs,
        out_specs=P(COL, ROW),
        check_vma=False,
    )
```

```python
import functools

import jax
import jax.numpy as jnp
from jax import lax
from jax.experimental import pallas as pl
from jax.experimental.pallas import tpu as pltpu
from jax.sharding import Mesh
from jax.sharding import PartitionSpec as P

NB = 128
HIGH = lax.Precision.HIGHEST
VMEM = pltpu.VMEM
SMEM = pltpu.SMEM
LIMIT = 16 * 1024 * 1024


def cost(microseconds):
    return pl.CostEstimate(
        flops=0, bytes_accessed=int(3.0e6 * microseconds), transcendentals=0
    )


def params(*semantics):
    return pltpu.CompilerParams(
        vmem_limit_bytes=LIMIT, dimension_semantics=semantics or None
    )


def parts_of(value, amount):
    parts = []
    for _ in range(amount):
        part = value.astype(jnp.bfloat16)
        parts.append(part)
        value = value - part.astype(jnp.float32)
    return jnp.concatenate(parts, axis=0)


def sum_parts(value, amount):
    rows = value.shape[0] // amount
    total = value[(amount - 1) * rows :]
    for index in reversed(range(amount - 1)):
        total = total + value[index * rows : (index + 1) * rows]
    return total


def chase_kernel(counts, offsets, band, vectors, out, places):
    slots, width = vectors.shape
    stored = band.shape[1]
    span = 2 * width
    low = offsets[0, 0]
    for slot in range(1, slots):
        low = jnp.minimum(low, offsets[0, slot])
    base = jnp.minimum((low // NB) * NB, stored - span)
    base = pl.multiple_of(base, NB)
    out[...] = band[...]
    window = band[:, pl.ds(base, span)]
    every = vectors[...]
    scaling = 2.0 / (jnp.sum(every * every, axis=1, keepdims=True) + 1e-06)
    for slot in range(slots):
        row = jnp.concatenate(
            [every[slot : slot + 1], jnp.zeros((1, span - width), jnp.float32)], axis=1
        )
        row = jnp.broadcast_to(row, (8, span))
        row = pltpu.roll(row, offsets[0, slot] - base, 1)
        row = jnp.concatenate([row] * (band.shape[0] // 8), axis=0)
        inner = jnp.sum(window * row, axis=1, keepdims=True)
        factor = jnp.where(slot < counts[0], scaling[slot : slot + 1], 0.0)
        window = window - (factor * inner) * row
    out[:, pl.ds(base, span)] = window
    part = places.shape[2]
    for index in range(places.shape[0]):
        places[index] = out[:, index * part : (index + 1) * part]


def chase(band, vectors, counts, offsets, places):
    rows, stored = band.shape
    return pl.pallas_call(
        chase_kernel,
        out_shape=[
            jax.ShapeDtypeStruct(band.shape, jnp.float32),
            jax.ShapeDtypeStruct((places, rows, stored // places), jnp.float32),
        ],
        in_specs=[
            pl.BlockSpec(memory_space=SMEM),
            pl.BlockSpec(memory_space=SMEM),
            pl.BlockSpec(memory_space=VMEM),
            pl.BlockSpec(memory_space=VMEM),
        ],
        out_specs=[pl.BlockSpec(memory_space=VMEM)] * 2,
        compiler_params=params(),
        cost_estimate=cost(4),
        name="chase",
    )(counts, offsets, band, vectors)


def place_product(mine, its, source, part):
    both = jnp.concatenate([mine[source], its[source]], axis=0)
    flat = part.reshape(part.shape[0] * part.shape[1], part.shape[2])
    return jnp.dot(parts_of(both, 3), flat, preferred_element_type=jnp.float32)


def near_kernel(place, mine, its, *rest, steps):
    pieces, (out, whole) = rest[: len(steps)], rest[len(steps) :]
    count = whole.shape[0]
    done = jnp.zeros((3 * out.shape[0], out.shape[1]), jnp.float32)
    for piece, step in zip(pieces, steps):
        step = jnp.where(place[0] == 0, step, -step)
        source = lax.rem(place[1] + step + count, count)
        part = piece[...]
        whole[source] = part
        done = done + place_product(mine, its, source, part)
    out[...] = sum_parts(done, 3)


def project_near(place, mine, its, pieces, steps):
    count, rows, _ = mine.shape
    shape = pieces[0].shape
    near = pl.BlockSpec(memory_space=VMEM)
    return pl.pallas_call(
        functools.partial(near_kernel, steps=steps),
        out_shape=[
            jax.ShapeDtypeStruct((2 * rows, shape[2]), jnp.float32),
            jax.ShapeDtypeStruct((count,) + shape, jnp.bfloat16),
        ],
        in_specs=[pl.BlockSpec(memory_space=SMEM)] + [near] * (2 + len(pieces)),
        out_specs=[near, near],
        compiler_params=params(),
        cost_estimate=cost(6),
        name="near",
    )(place, mine, its, *pieces)


def far_kernel(place, mine, its, before, piece, _, out, whole):
    count = whole.shape[0]
    rows = before.shape[0] // 2
    source = lax.rem(place[1] + count // 2, count)
    part = piece[...]
    whole[source] = part
    product = place_product(mine, its, source, part)
    done = before[...] + sum_parts(product, 3)
    zero = place[0] == 0
    own, other = done[:rows], done[rows:]
    even, odd = jnp.where(zero, own, other), jnp.where(zero, other, own)
    for index in range(out.shape[0] // 2):
        out[2 * index] = even
        out[2 * index + 1] = odd


def project_far(place, mine, its, before, piece, whole, copies):
    rows = mine.shape[1]
    near = pl.BlockSpec(memory_space=VMEM)
    return pl.pallas_call(
        far_kernel,
        out_shape=[
            jax.ShapeDtypeStruct((2 * copies, rows, whole.shape[3]), jnp.float32),
            jax.ShapeDtypeStruct(whole.shape, jnp.bfloat16),
        ],
        in_specs=[pl.BlockSpec(memory_space=SMEM)] + [near] * 5,
        out_specs=[near, near],
        input_output_aliases={5: 1},
        compiler_params=params(),
        cost_estimate=cost(2),
        name="far",
    )(place, mine, its, before, piece, whole)


TOP = 32767.0
SHIFT = 16


def encode(blocks):
    lane = lax.broadcasted_iota(jnp.int32, blocks[0].shape, 1)
    largest = jnp.zeros_like(blocks[0])
    for index, block in enumerate(blocks):
        size = jnp.max(jnp.abs(block), axis=1, keepdims=True)
        largest = jnp.where(lane == index, size, largest)
    exponent = jnp.floor(jnp.log2(jnp.maximum(largest, 1e-36)))
    exponent = jnp.clip(exponent, -118.0, 118.0)
    down = jnp.exp2(-exponent)
    mantissa = jnp.maximum(jnp.ceil(largest * down * 64.0), 1.0)
    back = (64.0 * TOP) / mantissa
    codes = []
    for index, block in enumerate(blocks):
        code = (block * down[:, index : index + 1]) * back[:, index : index + 1]
        code = jnp.clip(jnp.round(code), -TOP, TOP)
        codes.append(code.astype(jnp.int32).astype(jnp.int16))
    count = len(blocks)
    beside = jnp.where(lane < count, exponent, 0.0)
    moved = pltpu.roll(mantissa, SHIFT, 1)
    beside = jnp.where((lane >= SHIFT) & (lane < SHIFT + count), moved, beside)
    codes.append(beside.astype(jnp.int32).astype(jnp.int16))
    return codes


def decode_scales(beside):
    value = beside.astype(jnp.int32).astype(jnp.float32)
    lane = lax.broadcasted_iota(jnp.int32, value.shape, 1)
    mantissa = pltpu.roll(value, NB - SHIFT, 1)
    return (mantissa / (64.0 * TOP)) * jnp.exp2(jnp.where(lane < SHIFT, value, 0.0))


def update_kernel(
    core, shares, factor, chased, panel, panel_other, out
):
    low, high = shares[0], shares[1]
    for index in range(1, shares.shape[0] // 2):
        low = low + shares[2 * index]
        high = high + shares[2 * index + 1]
    product = lax.dot_general(
        jnp.concatenate([low, high], axis=1),
        factor[...],
        (((1,), (1,)), ((), ())),
        precision=HIGH,
        preferred_element_type=jnp.float32,
    )
    half = product.shape[1] // 2
    turned = jnp.concatenate([product[:, half:], product[:, :half]], axis=1)
    factored = parts_of(jnp.where(core[0] == 0, product, turned), 3)

    depth = out.shape[1] - 1
    chunk = depth * NB
    for index in range(out.shape[0]):
        lanes = pl.ds(index * chunk, chunk)
        both = jnp.concatenate([panel[lanes], panel_other[lanes]], axis=1)
        term = lax.dot_general(
            factored,
            both,
            (((1,), (1,)), ((), ())),
            preferred_element_type=jnp.float32,
        )
        value = chased[:, lanes] - sum_parts(term, 3)
        codes = encode([value[:, b * NB : (b + 1) * NB] for b in range(depth)])
        for b, code in enumerate(codes):
            out[index, b] = code


def update(core, shares, factor, chased, panel, panel_other, row_count):
    rows, stored = chased.shape
    depth = stored // (row_count * NB)
    near = pl.BlockSpec(memory_space=VMEM)
    return pl.pallas_call(
        update_kernel,
        out_shape=jax.ShapeDtypeStruct((row_count, depth + 1, rows, NB), jnp.int16),
        in_specs=[pl.BlockSpec(memory_space=SMEM)] + [near] * 5,
        out_specs=near,
        compiler_params=params(),
        cost_estimate=cost(6),
        name="update",
    )(core, shares, factor, chased, panel, panel_other)


def reorder_kernel(slots, table, isotope, blocks, out, triples, picked, staged, turned):
    sources, rows = blocks.shape[0], blocks.shape[2]
    depth = blocks.shape[1] - 1
    scales = [decode_scales(blocks[source, depth]) for source in range(sources)]

    def block(source, b):
        code = blocks[source, b].astype(jnp.int32).astype(jnp.float32)
        return code * scales[source][:, b : b + 1]

    groups = out.shape[1] // (3 * NB)
    here = lax.broadcasted_iota(jnp.int32, (3 * NB, 3 * NB), 0)
    there = lax.broadcasted_iota(jnp.int32, (3 * NB, 3 * NB), 1)
    spread = (here == 3 * (there % NB) + there // NB).astype(jnp.bfloat16)
    closed = (there == 3 * (here % NB) + here // NB).astype(jnp.bfloat16)

    kind = isotope[...]
    mass = jnp.full(kind.shape, 1.0, jnp.float32)
    for index in range(table.shape[0]):
        mass = jnp.where(kind == index, table[index], mass)
    scale = 1.0 / jnp.sqrt(mass)

    per = sources // 3
    tall_rows = 2 * rows
    for group in range(groups):
        b, q = group // per, group % per
        wide = jnp.concatenate([block(3 * q + k, b) for k in range(3)], axis=1)
        staged[group * tall_rows : (group + 1) * tall_rows, :] = parts_of(wide, 2)
    turned[...] = jnp.dot(staged[...], spread, preferred_element_type=jnp.float32)
    for group in range(groups):
        apart = sum_parts(turned[group * tall_rows : (group + 1) * tall_rows, :], 2)
        tall = jnp.concatenate(
            [apart[:, c * NB : (c + 1) * NB] for c in range(3)]
            + [jnp.zeros((NB - 3 * rows, NB), jnp.float32)],
            axis=0,
        )
        triples[group * NB : (group + 1) * NB, :] = tall.T

    unroll = 64

    def pick(step, carry):
        start = pl.multiple_of(step * unroll, unroll)
        for index in range(unroll):
            slot = slots[0, start + index]
            picked[pl.ds(start + index, 1), :] = triples[pl.ds(slot, 1), :]
        return carry

    lax.fori_loop(0, slots.shape[1] // unroll, pick, 0)

    for group in range(groups):
        tall = picked[group * NB : (group + 1) * NB, :].T
        factor = scale[group : group + 1, :]
        wide = jnp.concatenate(
            [tall[c * rows : (c + 1) * rows] * factor for c in range(3)], axis=1
        )
        staged[group * tall_rows : (group + 1) * tall_rows, :] = parts_of(wide, 2)
    turned[...] = jnp.dot(staged[...], closed, preferred_element_type=jnp.float32)
    for group in range(groups):
        out[:, group * 3 * NB : (group + 1) * 3 * NB] = sum_parts(
            turned[group * tall_rows : (group + 1) * tall_rows, :], 2
        )


def reorder(blocks, slots, isotope, table):
    sources, rows = blocks.shape[0], blocks.shape[2]
    stored = sources * (blocks.shape[1] - 1) * NB
    atoms = stored // 3
    return pl.pallas_call(
        reorder_kernel,
        out_shape=jax.ShapeDtypeStruct((rows, stored), jnp.float32),
        in_specs=[
            pl.BlockSpec(memory_space=SMEM),
            pl.BlockSpec(memory_space=SMEM),
            pl.BlockSpec(memory_space=VMEM),
            pl.BlockSpec(memory_space=VMEM),
        ],
        out_specs=pl.BlockSpec(memory_space=VMEM),
        scratch_shapes=[
            pltpu.VMEM((atoms, NB), jnp.float32),
            pltpu.VMEM((atoms, NB), jnp.float32),
            pltpu.VMEM((2 * rows * atoms // NB, 3 * NB), jnp.bfloat16),
            pltpu.VMEM((2 * rows * atoms // NB, 3 * NB), jnp.float32),
        ],
        compiler_params=params(),
        cost_estimate=cost(10),
        name="reorder",
    )(slots, table, isotope.reshape(-1, NB), blocks)


ROW = ("x", "z_lo")
COL = ("y", "z_hi", "core")
SIZES = (4, 3, 8, 4, 2)


def exchange(value, axes):
    return lax.all_to_all(value, axes, split_axis=0, concat_axis=0, tiled=True)


def other_core(value):
    return lax.ppermute(value, "core", [(0, 1), (1, 0)])


def shift(value, by):
    size = lax.axis_size("y")
    pairs = []
    for y in range(size):
        pairs.append((2 * y, 2 * ((y + by) % size)))
        pairs.append((2 * y + 1, 2 * ((y - by) % size) + 1))
    return lax.ppermute(value, ("y", "core"), pairs)


def gather_half(panel):
    half = panel.shape[1] // 2
    first = lax.axis_index("core") == 0
    got = other_core(panel)
    pair = jnp.where(
        first,
        jnp.concatenate([panel[:, :half], got[:, :half]]),
        jnp.concatenate([got[:, half:], panel[:, half:]]),
    )
    plane = lax.all_gather(pair, "z_hi", axis=0)
    up = down = plane
    pieces, steps = [plane], [0]
    for step in range(1, lax.axis_size("y") // 2):
        up, down = shift(up, 1), shift(down, -1)
        pieces += [up, down]
        steps += [-step, step]
    return pieces, steps, shift(up, 1)


def per_device(
    band_vectors,
    bulge_vectors,
    counts,
    offsets,
    panel_vectors,
    factor,
    atom_slot,
    isotope,
    mass_table,
):
    row_count = lax.axis_size(ROW)
    core = lax.axis_index("core").astype(jnp.int32)
    place = jnp.stack([core, lax.axis_index("y").astype(jnp.int32)])
    pieces, steps, far = gather_half(panel_vectors)
    chased, mine = chase(
        band_vectors, bulge_vectors[0], counts, offsets, lax.axis_size("y")
    )
    its = other_core(mine)
    before, whole = project_near(place, mine, its, pieces, steps)
    sums, panel = project_far(place, mine, its, before, far, whole, row_count)
    panel_other = other_core(panel)
    panel = panel.reshape(-1, panel.shape[3])
    panel_other = panel_other.reshape(panel.shape)
    shares = exchange(sums, ROW + ("core",))
    updated = update(place, shares, factor, chased, panel, panel_other, row_count)
    moved = exchange(updated, ROW)
    return reorder(moved, atom_slot, isotope, mass_table)


def solution(mesh):
    fine = Mesh(mesh.devices.reshape(SIZES), ROW + COL)
    in_specs = (
        P(COL, ROW),
        P(ROW, None, None),
        P(ROW),
        P(ROW, None),
        P(ROW + COL, None),
        P(),
        P(ROW, None),
        P(ROW),
        P(),
    )
    return jax.shard_map(
        per_device,
        mesh=fine,
        in_specs=in_specs,
        out_specs=P(COL, ROW),
        check_vma=False,
    )
```
